512 devices in a mesh: blk: 128 (over y_lo, x, z), grp: 4 (over y_hi, core).
Axes of the slice: x: 4, y: 8 (y_hi: 2, y_lo: 4; y = y_hi * 4 + y_lo), z: 8, core: 2. Of those that a mesh axis runs over, the one named last changes fastest.
Arguments:
- queries: bfloat16 [65536, 1024], P(('blk', 'grp')), may hold values from -16 to 16
- passages: bfloat16 [2048, 1024], P(('blk', 'grp')), may hold values from -16 to 16
- negatives: bfloat16 [458752, 1024], P(('blk', 'grp')), may hold values from -16 to 16
- neg_ids: int32 [65536, 7], P(('blk', 'grp')), may hold values from 0 to 458751, as said below
- positives: int32 [65536], P(('blk', 'grp')), may hold values from 0 to 2047
Outputs:
- grad_queries: float32 [65536, 1024], P(('blk', 'grp'))
- grad_passages: float32 [2048, 1024], P(('blk', 'grp'))
The draws below stay inside these ranges and needn't reach their ends.
Inputs may be any that keep to these rules, and one draw needn't show every extreme that they name: The row neg_ids[i, k] lies on a device of the same grp index as query i's device (rows are laid out 896 a device along blk+grp); of one device's queries at most 10 ids fall on any one device, and for every device there is some device on which exactly 10 of its ids fall.
All inputs are finite; a program needn't handle non-finite values.
Results may differ from the reference program's by a relative error of at most 0.0015.
Values may be sent and summed in bfloat16 or wider, within the bound.
A program may use at most 64 MiB of HBM per device.

```python
import math
import jax
import jax.numpy as jnp
from jax import lax

D = 1024
Q_DEV = 128
HARD = 7
H_DEV = 896
NQ = 65536
NP = 2048
NH = 458752
N_BLK = 128
N_GRP = 4
DEVICES = 512


def passage_base(key):
    return jnp.clip(jax.random.normal(jax.random.fold_in(key, 11), (NP, D), jnp.float32), -4.5, 4.5)


def target_gain():
    return math.sqrt(50.0 / math.sqrt(D))


def negative_rows(key, row_list):
    base_key = jax.random.fold_in(key, 12)

    def single_row(row_id):
        row_key = jax.random.fold_in(base_key, row_id)
        values = jnp.clip(jax.random.normal(row_key, (D,), jnp.float32), -4.5, 4.5)
        return values
    return jax.vmap(single_row)(row_list)


def id_lists(key):
    base_key = jax.random.fold_in(key, 13)
    per_device = Q_DEV * HARD
    base_count = per_device // N_BLK
    half_count = N_BLK // 2

    def per_owner(device):
        dev_key = jax.random.fold_in(base_key, device)
        ordering = jax.random.permutation(jax.random.fold_in(dev_key, 1), N_BLK)
        shifts = jax.random.randint(jax.random.fold_in(dev_key, 2), (half_count - 1,), 0, 4).astype(jnp.int32)
        paired = jnp.stack([shifts, -shifts], axis=1).reshape(-1)
        changes = jnp.concatenate([jnp.array([3], jnp.int32), paired, jnp.array([-3], jnp.int32)])
        counts = jnp.zeros((N_BLK,), jnp.int32).at[ordering].set(base_count + changes)
        owners = jnp.repeat(jnp.arange(N_BLK, dtype=jnp.int32), counts, total_repeat_length=per_device)
        owners = jax.random.permutation(jax.random.fold_in(dev_key, 3), owners)
        row_pick = jax.random.randint(jax.random.fold_in(dev_key, 4), (per_device,), 0, H_DEV).astype(jnp.int32)
        column = device % N_GRP
        return ((owners * N_GRP + column) * H_DEV + row_pick).reshape(Q_DEV, HARD)
    return jax.vmap(per_owner)(jnp.arange(DEVICES, dtype=jnp.int32)).reshape(NQ, HARD)


def drawn_rows():
    slots = jnp.arange(16, dtype=jnp.int32)
    return 2 * ((slots * 37 + 1) % (NP // 2))


def draw_neg_ids(key, part):
    return id_lists(key)


def draw_negatives(key, part):
    return negative_rows(key, jnp.arange(NH, dtype=jnp.int32)).astype(jnp.bfloat16)


def draw_passages(key, part):
    base = passage_base(key)
    gain = target_gain()
    index = jnp.arange(NP, dtype=jnp.int32)
    targets = drawn_rows()
    is_target = jnp.any(index[:, None] == targets[None, :], axis=1)
    is_partner = jnp.any((index - 1)[:, None] == targets[None, :], axis=1) & (index % 2 == 1)
    previous = jnp.roll(base, 1, axis=0)
    partner_rows = gain * (0.99 * previous + 0.1 * base)
    return jnp.where(is_partner[:, None], partner_rows, jnp.where(is_target[:, None], gain * base, base)).astype(jnp.bfloat16)


def draw_queries(key, part):
    own_key = jax.random.fold_in(key, 7)
    id_table = id_lists(key)
    hard_sum = jnp.zeros((NQ, D), jnp.float32)
    for column in range(HARD):
        hard_sum = hard_sum + negative_rows(key, id_table[:, column])
    noise = jnp.clip(jax.random.normal(own_key, (NQ, D), jnp.float32), -4.5, 4.5)
    mixed = 0.96 * noise + 0.1 * hard_sum
    base = passage_base(key)
    gain = target_gain()
    step_size = NQ // 16
    index = jnp.arange(NQ, dtype=jnp.int32)
    slot = jnp.minimum(index // step_size, 15)
    targets = drawn_rows()
    strengths = jnp.array([0.9, 1.15, 1.4], jnp.float32)[slot % 3]
    aligned = (strengths * gain)[:, None] * base[targets[slot]]
    return jnp.where((index % step_size == 0)[:, None], aligned, mixed).astype(jnp.bfloat16)


def touch_ends(values, key, low, largest):
    index_at = [jax.random.randint(jax.random.fold_in(key, axis), (), 0, length) for axis, length in enumerate(values.shape)]
    longest = values.shape.index(max(values.shape))
    next_to = index_at[:longest] + [(index_at[longest] + 1) % values.shape[longest]] + index_at[longest + 1:]
    return values.at[tuple(index_at)].set(low).at[tuple(next_to)].set(largest)


def setup_inputs(seed: int = 0) -> dict:
    splits = jax.random.split(jax.random.key(seed), 6)
    return {
        "queries": draw_queries(jax.random.fold_in(splits[5], 71), 0),
        "passages": draw_passages(jax.random.fold_in(splits[5], 71), 0),
        "negatives": draw_negatives(jax.random.fold_in(splits[5], 71), 0),
        "neg_ids": draw_neg_ids(jax.random.fold_in(splits[5], 71), 0),
        "positives": touch_ends(jax.random.randint(splits[4], (NQ,), 0, NP), jax.random.fold_in(splits[4], 1), 0, NP - 1).astype(jnp.int32),
    }


def reference(queries, passages, negatives, neg_ids, positives):
    score_scale = 3.0 / math.sqrt(D)
    block = Q_DEV * N_GRP
    count = NQ // block
    query_blocks = queries.reshape(count, block, D)
    id_blocks = neg_ids.reshape(count, block, HARD)
    answer_blocks = positives.reshape(count, block)
    pool_index = jnp.arange(NP, dtype=jnp.int32)

    def query_block(carried, inputs):
        block_q, block_ids, block_answer = inputs
        scores = jnp.dot(block_q, passages.T, preferred_element_type=jnp.float32) * score_scale
        hard_rows = negatives[block_ids]
        hard_scores = jnp.einsum('qd,qkd->qk', block_q.astype(jnp.float32), hard_rows.astype(jnp.float32)) * score_scale
        top_score = jnp.maximum(lax.optimization_barrier(jnp.max(scores, axis=1)), lax.optimization_barrier(jnp.max(hard_scores, axis=1)))
        totals = lax.optimization_barrier(jnp.sum(jnp.exp(scores - top_score[:, None]), axis=1)) + lax.optimization_barrier(jnp.sum(jnp.exp(hard_scores - top_score[:, None]), axis=1))
        lse = top_score + jnp.log(totals)
        answer_hot = (block_answer[:, None] == pool_index[None, :]).astype(jnp.float32)
        weights = (jnp.exp(scores - lse[:, None]) - answer_hot).astype(jnp.bfloat16)
        hard_weights = jnp.exp(hard_scores - lse[:, None]).astype(jnp.bfloat16)
        grad_block = jnp.dot(weights, passages, preferred_element_type=jnp.float32)
        grad_block = grad_block + jnp.einsum('qk,qkd->qd', hard_weights.astype(jnp.float32), hard_rows.astype(jnp.float32))
        carried = carried + jnp.dot(weights.T, block_q, preferred_element_type=jnp.float32)
        return (carried, grad_block * score_scale)
    passage_sum, grad_blocks = lax.scan(query_block, jnp.zeros((NP, D), jnp.float32), (query_blocks, id_blocks, answer_blocks))
    return (grad_blocks.reshape(NQ, D), passage_sum * score_scale)
```

```python
import functools
import math

import jax
import jax.numpy as jnp
from jax import lax
from jax.experimental import pallas as pl
from jax.experimental.pallas import tpu as pltpu
from jax.sharding import PartitionSpec as P

MESH = pl.DeviceIdType.MESH
F32, BF16, I32 = jnp.float32, jnp.bfloat16, jnp.int32

NX, NY, NZ, NYL = 4, 8, 8, 4
NB = 128
MUL, INV = 37, 45
CAP = 10
Q, D, HARD, ROWS = 128, 1024, 7, 896
C8 = D // 128
SLAB = CAP * C8
GROUPS = 8
PER = NB // GROUPS
SLOTS = NB * CAP
NP = 2048
SCALE = 3.0 / math.sqrt(D)
NEG = -1e30


def device(x, y, z, core):
    return (((y % NYL) * NX + x) * NZ + z, (y // NYL) * 2 + core)


def rcopy(src, dst, send, recv, dev):
    return pltpu.make_async_remote_copy(
        src_ref=src, dst_ref=dst, send_sem=send, recv_sem=recv, device_id=dev, device_id_type=MESH
    )


def nt(left, right):
    return lax.dot_general(left, right, (((1,), (1,)), ((), ())), preferred_element_type=F32)


def mm(left, right):
    return lax.dot_general(left, right, (((1,), (0,)), ((), ())), preferred_element_type=F32)


def iota(shape, dim):
    return lax.broadcasted_iota(I32, shape, dim)


def requests(ids_ref, req, slots):
    mb = lax.axis_index("blk")
    yl, x, z = mb // (NX * NZ), (mb // NZ) % NX, mb % NZ

    lane = iota((Q, 128), 1)
    lower = (iota((Q, Q), 0) > iota((Q, Q), 1)).astype(F32).astype(BF16)
    base = jnp.zeros((1, 128), F32)
    want_hi = jnp.zeros((NB, 128), F32)
    want_lo = jnp.zeros((NB, 128), F32)
    slot_cols = jnp.full((Q, 128), -1.0, F32)
    for k in range(HARD):
        ids = ids_ref[:, k:k + 1]
        dev = jnp.floor((ids.astype(F32) + 0.5) * (1.0 / ROWS)).astype(I32)
        row = ids - dev * ROWS
        owner = dev >> 2
        off = (
            (((yl - (owner >> 5)) & 3) << 5)
            | (((x - ((owner >> 3) & 3)) & 3) << 3)
            | ((z - (owner & 7)) & 7)
        )
        step = (off * INV) & (NB - 1)
        hot = (lane == step).astype(F32)
        rank = jnp.sum(hot * (mm(lower, hot.astype(BF16)) + base), axis=1, keepdims=True)
        base = base + jnp.sum(hot, axis=0, keepdims=True)
        slot_cols = jnp.where(lane == k, step.astype(F32) * CAP + rank, slot_cols)
        at_rank = (lane.astype(F32) == rank).astype(F32)
        hot_t = jnp.transpose(hot).astype(BF16)
        want_hi = want_hi + mm(hot_t, (at_rank * (row >> 3).astype(F32)).astype(BF16))
        want_lo = want_lo + mm(hot_t, (at_rank * (row & 7).astype(F32)).astype(BF16))
    want = (want_hi * 8.0 + want_lo).astype(I32)
    req[...] = want.reshape(NB, 1, 128)
    slots[...] = jnp.transpose(slot_cols).astype(I32)


def kernel(
    req, slots, pos_ref, pas_ref, q_ref, neg_ref,
    gq_ref, gp_ref,
    reqin, idsm, tab, g, f, fs, fn, st, hs, pst, pmine, zbuf, zf, pall,
    wt, gpb, rc, r1x, r1a, ax, aa, r2x, r2a, a3, r3,
    s_req, s_row, s_ag, r_req, r_row, r_ag, s_rc, r_rc, s_1, r_1, s_2, r_2, s_3, r_3, s_loc,
):
    mb = lax.axis_index("blk")
    mg = lax.axis_index("grp")
    yl, x, z = mb // (NX * NZ), (mb // NZ) % NX, mb % NZ
    yh, core = mg // 2, mg % 2
    y = yh * NYL + yl

    def shifted(step, sign):
        k = (step * MUL) % NB
        ky, kx, kz = k // (NX * NZ), (k // NZ) % NX, k % NZ
        py = (yl + NYL + sign * ky) % NYL
        px = (x + NX + sign * kx) % NX
        pz = (z + NZ + sign * kz) % NZ
        return ((py * NX + px) * NZ + pz, mg)

    sibling = device(x, y, z, 1 - core)

    barrier = pltpu.get_barrier_semaphore()

    def greet(step, _):
        pl.semaphore_signal(barrier, inc=1, device_id=shifted(step, 1), device_id_type=MESH)
        return 0

    lax.fori_loop(1, NB, greet, 0)
    for i in range(NYL):
        other = device(x, (1 - yh) * NYL + i, z, core)
        pl.semaphore_signal(barrier, inc=1, device_id=other, device_id_type=MESH)
    pl.semaphore_signal(barrier, inc=1, device_id=sibling, device_id_type=MESH)

    for c in range(C8):
        pst[pl.ds(c, 4, stride=C8), :] = pas_ref[:, c * 128:(c + 1) * 128].astype(F32)
    own = pst[...].astype(BF16)
    pmine[...] = own
    zbuf[z] = own

    pl.semaphore_wait(barrier, NB - 1 + NYL + 1)

    def ask(step, _):
        rcopy(req.at[step], reqin.at[step], s_req, r_req, shifted(step, -1)).start()
        return 0

    lax.fori_loop(1, NB, ask, 0)
    reqin[0] = req[0]

    for i in range(1, NZ):
        to = device(x, y, (z + i) % NZ, core)
        rcopy(pmine, zbuf.at[z], s_ag.at[0], r_ag.at[0], to).start()

    flat = tab.reshape(ROWS * C8, 128)
    for t in range(ROWS // 128):
        for c in range(C8):
            part = neg_ref[t * 128:(t + 1) * 128, c * 128:(c + 1) * 128].astype(F32)
            flat[pl.ds(t * 1024 + c, 128, stride=C8), :] = part

    rcopy(zbuf.at[pl.ds(0, NZ - 1)], zbuf.at[pl.ds(0, NZ - 1)], s_ag.at[0], r_ag.at[0], sibling).wait_recv()
    zf[...] = zbuf[...].reshape(NZ * 32, 128).astype(F32)
    mine = pl.multiple_of(((core * NX + x) * NY + y) * 32, 32)
    for c in range(C8):
        pall[pl.ds(mine, 32), c * 128:(c + 1) * 128] = zf[pl.ds(c, 32, stride=C8), :].astype(BF16)

    for i in range(1, NY):
        to = device(x, (y + i) % NY, z, core)
        block = pall.at[pl.ds(mine, 32)]
        rcopy(block, block, s_ag.at[1], r_ag.at[1], to).start()

    rcopy(reqin.at[pl.ds(0, NB - 1)], reqin.at[pl.ds(0, NB - 1)], s_req, r_req, sibling).wait_recv()
    local = pltpu.make_async_copy(reqin, idsm, s_loc)
    local.start()
    local.wait()

    def pick(step, dst):
        at = pl.multiple_of(step * SLAB, 16)
        for j in range(CAP // 2):
            pair = jnp.concatenate([tab[idsm[step, 0, 2 * j]], tab[idsm[step, 0, 2 * j + 1]]], axis=0)
            dst[pl.ds(at + 16 * j, 16), :] = pair.astype(BF16)

    def answer(step, _):
        pick(step, g)
        at = pl.multiple_of(step * SLAB, 16)
        rcopy(
            g.at[pl.ds(at, SLAB)], f.at[pl.ds(at, SLAB)], s_row, r_row.at[step // PER], shifted(step, 1)
        ).start()
        return 0

    lax.fori_loop(1, NB, answer, 0)
    pick(0, f)

    rcopy(pall.at[pl.ds(0, 224)], pall.at[pl.ds(0, 224)], s_ag.at[1], r_ag.at[1], sibling).wait_recv()
    for i in range(1, NX):
        to = device((x + i) % NX, y, z, core)
        block = pall.at[pl.ds(pl.multiple_of((core * NX + x) * 256, 256), 256)]
        rcopy(block, block, s_ag.at[2], r_ag.at[2], to).start()
    rcopy(pall.at[pl.ds(0, 768)], pall.at[pl.ds(0, 768)], s_ag.at[2], r_ag.at[2], sibling).wait_recv()
    half = pall.at[pl.ds(pl.multiple_of(core * 1024, 1024), 1024)]
    rcopy(half, half, s_ag.at[3], r_ag.at[3], sibling).start()
    rcopy(half, half, s_ag.at[3], r_ag.at[3], sibling).wait_recv()

    def score(t, top):
        at = pl.multiple_of(t * 256, 256)
        part = nt(pall[pl.ds(at, 256), :], q_ref[...]) * SCALE
        st[pl.ds(at, 256), :] = part
        return jnp.maximum(top, jnp.max(part, axis=0, keepdims=True))

    top = lax.fori_loop(0, NP // 256, score, jnp.full((1, Q), NEG, F32))

    def hard(group, top):
        at = pl.multiple_of(group * PER * SLAB, PER * SLAB)
        row0 = pl.multiple_of(group * PER * CAP, PER * CAP)
        fs[...] = f[pl.ds(at, PER * SLAB), :].astype(F32)
        for c in range(C8):
            fn[pl.ds(row0, PER * CAP), c * 128:(c + 1) * 128] = fs[
                pl.ds(c, PER * CAP, stride=C8), :
            ].astype(BF16)
        part = nt(fn[pl.ds(row0, PER * CAP), :], q_ref[...]) * SCALE
        number = iota((PER * CAP, Q), 0) + row0
        taken = number == slots[0:1, :]
        for k in range(1, HARD):
            taken = taken | (number == slots[k:k + 1, :])
        part = jnp.where(taken, part, NEG)
        hs[pl.ds(row0, PER * CAP), :] = part
        return jnp.maximum(top, jnp.max(part, axis=0, keepdims=True))

    for group in range(GROUPS):
        n = PER - (1 if group == 0 else 0)
        ref = f.at[pl.ds(0, n * SLAB)]
        rcopy(ref, ref, s_row, r_row.at[group], sibling).wait_recv()
        top = hard(group, top)

    total = jnp.sum(jnp.exp(st[...] - top), axis=0, keepdims=True) + jnp.sum(
        jnp.exp(hs[...] - top), axis=0, keepdims=True
    )
    lse = top + jnp.log(total)

    p = pos_ref[...]
    answer_slot = (
        (((p >> 2) & 1) << 10)
        | (((p >> 7) & 3) << 8)
        | (((p >> 3) & 1) << 7)
        | (((p >> 9) & 3) << 5)
        | (((p >> 4) & 7) << 2)
        | (p & 3)
    )
    there = iota((256, 256), 0)
    source = (((there >> 2) & 7) << 5) | ((there >> 5) << 2) | (there & 3)
    swap = (iota((256, 256), 1) == source).astype(F32).astype(BF16)
    for t in range(NP // 256):
        rows = slice(t * 256, (t + 1) * 256)
        hit = (iota((256, Q), 0) + t * 256 == answer_slot).astype(F32)
        w = jnp.exp(st[rows, :] - lse) - hit
        st[rows, :] = w
        w = w.astype(BF16)
        wt[0, rows, :] = w
        wt[1, rows, :] = mm(swap, w).astype(BF16)

    def grads(j, side):
        def one(i, _):
            at = pl.multiple_of(side * 1024 + i * 256, 256)
            part = mm(wt[j // 2, pl.ds(at, 256), :], q_ref[:, j * 256:(j + 1) * 256])
            gpb[j, side, i] = part.reshape(8, 32, 256)
            return 0

        lax.fori_loop(0, NX, one, 0)

    for j in range(4):
        grads(j, 1 - core)
        rcopy(gpb.at[j, 1 - core], rc.at[j], s_rc.at[j], r_rc.at[j], sibling).start()
    for j in range(4):
        grads(j, core)

    def along(axis, i):
        return (
            device((x + i) % NX, y, z, core) if axis == "x"
            else device(x, (y + i) % NY, z, core) if axis == "y"
            else device(x, y, (z + i) % NZ, core)
        )

    where = {"x": x, "y": y, "z": z}
    size = {"x": NX, "y": NY, "z": NZ}

    for j in range(4):
        o, first_x = j // 2, j % 2 == 0
        a = "yz"[o]
        rcopy(gpb.at[j, 1 - core], rc.at[j], s_rc.at[j], r_rc.at[j], sibling).wait_recv()

        def add(i, _, j=j):
            gpb[j, core, i] = gpb[j, core, i] + rc[j, i]
            return 0

        lax.fori_loop(0, NX, add, 0)
        if first_x:
            for i in range(1, NX):
                rcopy(
                    gpb.at[j, core, (x + i) % NX], r1x.at[o, i - 1], s_1.at[j], r_1.at[j], along("x", i)
                ).start()
        else:
            for i in range(1, 8):
                rcopy(
                    gpb.at[j, core, :, (where[a] + i) % 8], r1a.at[o, i - 1], s_1.at[j], r_1.at[j], along(a, i)
                ).start()

    for half_at in range(2):
        cols = slice(half_at * 512, (half_at + 1) * 512)

        def passages(t, acc, cols=cols):
            at = pl.multiple_of(t * 256, 256)
            w = jnp.transpose(st[pl.ds(at, 256), :]).astype(BF16)
            return acc + mm(w, pall[pl.ds(at, 256), cols])

        def negatives(t, acc, cols=cols):
            at = pl.multiple_of(t * 256, 256)
            w = jnp.transpose(jnp.exp(hs[pl.ds(at, 256), :] - lse)).astype(BF16)
            return acc + mm(w, fn[pl.ds(at, 256), cols])

        acc = lax.fori_loop(0, NP // 256, passages, jnp.zeros((Q, 512), F32))
        acc = lax.fori_loop(0, SLOTS // 256, negatives, acc)
        gq_ref[:, cols] = acc * SCALE

    for j in range(4):
        o, first_x = j // 2, j % 2 == 0
        a = "yz"[o]
        if first_x:
            rcopy(r1x.at[o], r1x.at[o], s_1.at[j], r_1.at[j], sibling).wait_recv()
            acc = gpb[j, core, x]
            for i in range(NX - 1):
                acc = acc + r1x[o, i]
            ax[o] = acc
            for i in range(1, 8):
                rcopy(
                    ax.at[o, (where[a] + i) % 8], r2a.at[o, i - 1], s_2.at[j], r_2.at[j], along(a, i)
                ).start()
        else:
            rcopy(r1a.at[o], r1a.at[o], s_1.at[j], r_1.at[j], sibling).wait_recv()
            for i in range(NX):
                acc = gpb[j, core, i, where[a]]
                for n in range(7):
                    acc = acc + r1a[o, n, i]
                aa[o, i] = acc
            for i in range(1, NX):
                rcopy(
                    aa.at[o, (x + i) % NX], r2x.at[o, i - 1], s_2.at[j], r_2.at[j], along("x", i)
                ).start()

    for j in range(4):
        o, first_x = j // 2, j % 2 == 0
        a, b = "yz"[o], "zy"[o]
        if first_x:
            rcopy(r2a.at[o], r2a.at[o], s_2.at[j], r_2.at[j], sibling).wait_recv()
            acc = ax[o, where[a]]
            for i in range(7):
                acc = acc + r2a[o, i]
        else:
            rcopy(r2x.at[o], r2x.at[o], s_2.at[j], r_2.at[j], sibling).wait_recv()
            acc = aa[o, x]
            for i in range(NX - 1):
                acc = acc + r2x[o, i]
        for i in range(8):
            a3[j, i] = acc[i * 4:(i + 1) * 4, :]
        for i in range(1, 8):
            rcopy(
                a3.at[j, (where[b] + i) % 8], r3.at[j, i - 1], s_3.at[j], r_3.at[j], along(b, i)
            ).start()

    for j in range(4):
        b = "zy"[j // 2]
        rcopy(r3.at[j], r3.at[j], s_3.at[j], r_3.at[j], sibling).wait_recv()
        acc = a3[j, where[b]]
        for i in range(7):
            acc = acc + r3[j, i]
        gp_ref[:, j * 256:(j + 1) * 256] = acc * SCALE

    def left(ref, sem):
        rcopy(ref, ref, sem, sem, sibling).wait_send()

    left(reqin.at[pl.ds(0, NB - 1)], s_req)
    left(f.at[pl.ds(0, (NB - 1) * SLAB)], s_row)
    left(zbuf.at[pl.ds(0, NZ - 1)], s_ag.at[0])
    left(pall.at[pl.ds(0, 224)], s_ag.at[1])
    left(pall.at[pl.ds(0, 768)], s_ag.at[2])
    left(pall.at[pl.ds(0, 1024)], s_ag.at[3])
    for j in range(4):
        o, first_x = j // 2, j % 2 == 0
        left(rc.at[j], s_rc.at[j])
        left(r1x.at[o] if first_x else r1a.at[o], s_1.at[j])
        left(r2a.at[o] if first_x else r2x.at[o], s_2.at[j])
        left(r3.at[j], s_3.at[j])


def shards(queries, passages, negatives, neg_ids, positives):
    vmem = pl.BlockSpec(memory_space=pltpu.VMEM)
    dma = pltpu.SemaphoreType.DMA
    req, slots = pl.pallas_call(
        requests,
        out_shape=(
            jax.ShapeDtypeStruct((NB, 1, 128), I32),
            jax.ShapeDtypeStruct((128, Q), I32),
        ),
        in_specs=[vmem],
        out_specs=(vmem, vmem),
    )(neg_ids)
    return pl.pallas_call(
        kernel,
        out_shape=(
            jax.ShapeDtypeStruct((Q, D), F32),
            jax.ShapeDtypeStruct((4, D), F32),
        ),
        in_specs=[vmem] * 6,
        out_specs=(vmem, vmem),
        scratch_shapes=[
            pltpu.VMEM((NB, 1, 128), I32),
            pltpu.SMEM((NB, 1, 128), I32),
            pltpu.VMEM((ROWS, C8, 128), F32),
            pltpu.VMEM((NB * SLAB, 128), BF16),
            pltpu.VMEM((NB * SLAB, 128), BF16),
            pltpu.VMEM((PER * SLAB, 128), F32),
            pltpu.VMEM((SLOTS, D), BF16),
            pltpu.VMEM((NP, Q), F32),
            pltpu.VMEM((SLOTS, Q), F32),
            pltpu.VMEM((32, 128), F32),
            pltpu.VMEM((32, 128), BF16),
            pltpu.VMEM((NZ, 32, 128), BF16),
            pltpu.VMEM((NZ * 32, 128), F32),
            pltpu.VMEM((NP, D), BF16),
            pltpu.VMEM((2, NP, Q), BF16),
            pltpu.VMEM((4, 2, NX, 8, 32, 256), F32),
            pltpu.VMEM((4, NX, 8, 32, 256), F32),
            pltpu.VMEM((2, NX - 1, 8, 32, 256), F32),
            pltpu.VMEM((2, 7, NX, 32, 256), F32),
            pltpu.VMEM((2, 8, 32, 256), F32),
            pltpu.VMEM((2, NX, 32, 256), F32),
            pltpu.VMEM((2, NX - 1, 32, 256), F32),
            pltpu.VMEM((2, 7, 32, 256), F32),
            pltpu.VMEM((4, 8, 4, 256), F32),
            pltpu.VMEM((4, 7, 4, 256), F32),
            dma, dma, dma((4,)), dma, dma((GROUPS,)), dma((4,)),
            dma((4,)), dma((4,)), dma((4,)), dma((4,)),
            dma((4,)), dma((4,)), dma((4,)), dma((4,)), dma,
        ],
        compiler_params=pltpu.CompilerParams(
            collective_id=0, has_side_effects=True, vmem_limit_bytes=58 * 1024 * 1024
        ),
        cost_estimate=pl.CostEstimate(flops=4 * Q * NP * D * 2, bytes_accessed=1 << 24, transcendentals=0),
    )(req, slots, positives.reshape(1, Q), passages, queries, negatives)


def solution(mesh):
    rows = P(("blk", "grp"), None)
    return jax.shard_map(
        shards,
        mesh=mesh,
        in_specs=(rows, rows, rows, rows, P(("blk", "grp"))),
        out_specs=(rows, rows),
        check_vma=False,
    )
```

```python
import functools
import math

import jax
import jax.numpy as jnp
from jax import lax
from jax.experimental import pallas as pl
from jax.experimental.pallas import tpu as pltpu
from jax.sharding import PartitionSpec as P

MESH = pl.DeviceIdType.MESH
F32, BF16, I32 = jnp.float32, jnp.bfloat16, jnp.int32

NX, NY, NZ, NYL = 4, 8, 8, 4
NB = 128
MUL, INV = 37, 45
CAP = 10
Q, D, HARD, ROWS = 128, 1024, 7, 896
C8 = D // 128
SLAB = CAP * C8
GROUPS = 8
PER = NB // GROUPS
SLOTS = NB * CAP
NP = 2048
SCALE = 3.0 / math.sqrt(D)
NEG = -1e30


def device(x, y, z, core):
    return (((y % NYL) * NX + x) * NZ + z, (y // NYL) * 2 + core)


def rcopy(src, dst, send, recv, dev):
    return pltpu.make_async_remote_copy(
        src_ref=src, dst_ref=dst, send_sem=send, recv_sem=recv, device_id=dev, device_id_type=MESH
    )


def nt(left, right):
    return lax.dot_general(left, right, (((1,), (1,)), ((), ())), preferred_element_type=F32)


def mm(left, right):
    return lax.dot_general(left, right, (((1,), (0,)), ((), ())), preferred_element_type=F32)


def iota(shape, dim):
    return lax.broadcasted_iota(I32, shape, dim)


def requests(ids_ref, req, slots):
    mb = lax.axis_index("blk")

    lane = iota((Q, 128), 1)
    lower = (iota((Q, Q), 0) > iota((Q, Q), 1)).astype(F32).astype(BF16)
    base = jnp.zeros((1, 128), F32)
    want_hi = jnp.zeros((NB, 128), F32)
    want_lo = jnp.zeros((NB, 128), F32)
    slot_cols = jnp.full((Q, 128), -1.0, F32)
    for k in range(HARD):
        ids = ids_ref[:, k:k + 1]
        dev = jnp.floor((ids.astype(F32) + 0.5) * (1.0 / ROWS)).astype(I32)
        row = ids - dev * ROWS
        owner = dev >> 2
        off = owner ^ mb
        step = (off * INV) & (NB - 1)
        hot = (lane == step).astype(F32)
        rank = jnp.sum(hot * (mm(lower, hot.astype(BF16)) + base), axis=1, keepdims=True)
        base = base + jnp.sum(hot, axis=0, keepdims=True)
        slot_cols = jnp.where(lane == k, step.astype(F32) * CAP + rank, slot_cols)
        at_rank = (lane.astype(F32) == rank).astype(F32)
        hot_t = jnp.transpose(hot).astype(BF16)
        want_hi = want_hi + mm(hot_t, (at_rank * (row >> 3).astype(F32)).astype(BF16))
        want_lo = want_lo + mm(hot_t, (at_rank * (row & 7).astype(F32)).astype(BF16))
    want = (want_hi * 8.0 + want_lo).astype(I32)
    req[...] = want.reshape(NB, 1, 128)
    slots[...] = jnp.transpose(slot_cols).astype(I32)


def kernel(
    req, slots, pos_ref, pas_ref, q_ref, neg_ref,
    gq_ref, gp_ref,
    reqin, idsm, tab, g, f, fs, fn, st, hs, pst, pmine, zbuf, zf, pall,
    wt, gpb, rc, r1x, r1a, ax, aa, r2x, r2a, a3, r3,
    s_req, s_row, s_ag, r_req, r_row, r_ag, s_rc, r_rc, s_1, r_1, s_2, r_2, s_3, r_3, s_loc,
):
    mb = lax.axis_index("blk")
    mg = lax.axis_index("grp")
    yl, x, z = mb // (NX * NZ), (mb // NZ) % NX, mb % NZ
    yh, core = mg // 2, mg % 2
    y = yh * NYL + yl

    def partner(step):
        return (mb ^ ((step * MUL) & (NB - 1)), mg)

    sibling = device(x, y, z, 1 - core)

    barrier = pltpu.get_barrier_semaphore()

    def greet(step, _):
        pl.semaphore_signal(barrier, inc=1, device_id=partner(step), device_id_type=MESH)
        return 0

    lax.fori_loop(1, NB, greet, 0)
    for i in range(NYL):
        other = device(x, (1 - yh) * NYL + i, z, core)
        pl.semaphore_signal(barrier, inc=1, device_id=other, device_id_type=MESH)
    pl.semaphore_signal(barrier, inc=1, device_id=sibling, device_id_type=MESH)

    for c in range(C8):
        pst[pl.ds(c, 4, stride=C8), :] = pas_ref[:, c * 128:(c + 1) * 128].astype(F32)
    own = pst[...].astype(BF16)
    pmine[...] = own
    zbuf[z] = own

    pl.semaphore_wait(barrier, NB - 1 + NYL + 1)

    def ask(step, _):
        rcopy(req.at[step], reqin.at[step], s_req, r_req, partner(step)).start()
        return 0

    lax.fori_loop(1, NB, ask, 0)
    reqin[0] = req[0]

    for i in range(1, NZ):
        to = device(x, y, (z + i) % NZ, core)
        rcopy(pmine, zbuf.at[z], s_ag.at[0], r_ag.at[0], to).start()

    flat = tab.reshape(ROWS * C8, 128)
    for t in range(ROWS // 128):
        for c in range(C8):
            part = neg_ref[t * 128:(t + 1) * 128, c * 128:(c + 1) * 128].astype(F32)
            flat[pl.ds(t * 1024 + c, 128, stride=C8), :] = part

    rcopy(zbuf.at[pl.ds(0, NZ - 1)], zbuf.at[pl.ds(0, NZ - 1)], s_ag.at[0], r_ag.at[0], sibling).wait_recv()
    zf[...] = zbuf[...].reshape(NZ * 32, 128).astype(F32)
    mine = pl.multiple_of(((core * NX + x) * NY + y) * 32, 32)
    for c in range(C8):
        pall[pl.ds(mine, 32), c * 128:(c + 1) * 128] = zf[pl.ds(c, 32, stride=C8), :].astype(BF16)

    for i in range(1, NY):
        to = device(x, (y + i) % NY, z, core)
        block = pall.at[pl.ds(mine, 32)]
        rcopy(block, block, s_ag.at[1], r_ag.at[1], to).start()

    rcopy(reqin.at[pl.ds(0, NB - 1)], reqin.at[pl.ds(0, NB - 1)], s_req, r_req, sibling).wait_recv()
    local = pltpu.make_async_copy(reqin, idsm, s_loc)
    local.start()
    local.wait()

    def pick(step, dst):
        at = pl.multiple_of(step * SLAB, 16)
        for j in range(CAP // 2):
            pair = jnp.concatenate([tab[idsm[step, 0, 2 * j]], tab[idsm[step, 0, 2 * j + 1]]], axis=0)
            dst[pl.ds(at + 16 * j, 16), :] = pair.astype(BF16)

    def answer(step, _):
        pick(step, g)
        at = pl.multiple_of(step * SLAB, 16)
        rcopy(
            g.at[pl.ds(at, SLAB)], f.at[pl.ds(at, SLAB)], s_row, r_row.at[step // PER], partner(step)
        ).start()
        return 0

    lax.fori_loop(1, NB, answer, 0)
    pick(0, f)

    rcopy(pall.at[pl.ds(0, 224)], pall.at[pl.ds(0, 224)], s_ag.at[1], r_ag.at[1], sibling).wait_recv()
    right, left_x = device((x + 1) % NX, y, z, core), device((x + NX - 1) % NX, y, z, core)

    def slab(at, rows, extra=0):
        return pall.at[pl.ds(pl.multiple_of((core * NX + at) * 256 + extra, 128), rows)]

    for n, to in ((0, right), (1, left_x)):
        rcopy(slab(x, 256), slab(x, 256), s_ag.at[2 + n], r_ag.at[2 + n], to).start()
    for n, to in ((0, right), (1, left_x)):
        came = (x + NX - 1) % NX if n == 0 else (x + 1) % NX
        rcopy(slab(came, 256), slab(came, 256), s_ag.at[2 + n], r_ag.at[2 + n], to).wait_recv()
        part = slab(came, 128, 128 * n)
        rcopy(part, part, s_ag.at[4 + n], r_ag.at[4 + n], to).start()
    for n in range(2):
        part = slab((x + 2) % NX, 128, 128 * n)
        rcopy(part, part, s_ag.at[4 + n], r_ag.at[4 + n], sibling).wait_recv()
    half = pall.at[pl.ds(pl.multiple_of(core * 1024, 1024), 1024)]
    rcopy(half, half, s_ag.at[6], r_ag.at[6], sibling).start()
    rcopy(half, half, s_ag.at[6], r_ag.at[6], sibling).wait_recv()

    def score(t, top):
        at = pl.multiple_of(t * 256, 256)
        part = nt(pall[pl.ds(at, 256), :], q_ref[...]) * SCALE
        st[pl.ds(at, 256), :] = part
        return jnp.maximum(top, jnp.max(part, axis=0, keepdims=True))

    pool_top = lax.fori_loop(0, NP // 256, score, jnp.full((1, Q), NEG, F32))

    def raise_(t, total):
        at = pl.multiple_of(t * 256, 256)
        part = jnp.exp(st[pl.ds(at, 256), :] - pool_top)
        st[pl.ds(at, 256), :] = part
        return total + jnp.sum(part, axis=0, keepdims=True)

    pool_total = lax.fori_loop(0, NP // 256, raise_, jnp.zeros((1, Q), F32))
    top = pool_top

    def hard(group, top):
        at = pl.multiple_of(group * PER * SLAB, PER * SLAB)
        row0 = pl.multiple_of(group * PER * CAP, PER * CAP)
        fs[...] = f[pl.ds(at, PER * SLAB), :].astype(F32)
        for c in range(C8):
            fn[pl.ds(row0, PER * CAP), c * 128:(c + 1) * 128] = fs[
                pl.ds(c, PER * CAP, stride=C8), :
            ].astype(BF16)
        part = nt(fn[pl.ds(row0, PER * CAP), :], q_ref[...]) * SCALE
        number = iota((PER * CAP, Q), 0) + row0
        taken = number == slots[0:1, :]
        for k in range(1, HARD):
            taken = taken | (number == slots[k:k + 1, :])
        part = jnp.where(taken, part, NEG)
        hs[pl.ds(row0, PER * CAP), :] = part
        return jnp.maximum(top, jnp.max(part, axis=0, keepdims=True))

    for group in range(GROUPS):
        n = PER - (1 if group == 0 else 0)
        ref = f.at[pl.ds(0, n * SLAB)]
        rcopy(ref, ref, s_row, r_row.at[group], sibling).wait_recv()
        top = hard(group, top)

    total = pool_total * jnp.exp(pool_top - top) + jnp.sum(jnp.exp(hs[...] - top), axis=0, keepdims=True)
    lse = top + jnp.log(total)
    factor = jnp.exp(pool_top - lse)

    p = pos_ref[...]
    answer_slot = (
        (((p >> 2) & 1) << 10)
        | (((p >> 7) & 3) << 8)
        | (((p >> 3) & 1) << 7)
        | (((p >> 9) & 3) << 5)
        | (((p >> 4) & 7) << 2)
        | (p & 3)
    )
    there = iota((256, 256), 0)
    source = (((there >> 2) & 7) << 5) | ((there >> 5) << 2) | (there & 3)
    swap = (iota((256, 256), 1) == source).astype(F32).astype(BF16)

    def weigh(side):
        def one(i, _):
            at = pl.multiple_of(side * 1024 + i * 256, 256)
            hit = (iota((256, Q), 0) + at == answer_slot).astype(F32)
            w = st[pl.ds(at, 256), :] * factor - hit
            st[pl.ds(at, 256), :] = w
            w = w.astype(BF16)
            wt[0, pl.ds(at, 256), :] = w
            wt[1, pl.ds(at, 256), :] = mm(swap, w).astype(BF16)
            return 0

        lax.fori_loop(0, NX, one, 0)

    def grads(j, side):
        def one(i, _):
            at = pl.multiple_of(side * 1024 + i * 256, 256)
            part = mm(wt[j // 2, pl.ds(at, 256), :], q_ref[:, j * 256:(j + 1) * 256])
            gpb[j, side, i] = part.reshape(8, 32, 256)
            return 0

        lax.fori_loop(0, NX, one, 0)

    order = (1, 3, 0, 2)
    weigh(1 - core)
    for j in order:
        grads(j, 1 - core)
        rcopy(gpb.at[j, 1 - core], rc.at[j], s_rc.at[j], r_rc.at[j], sibling).start()
    weigh(core)
    for j in order:
        grads(j, core)

    def along(axis, i):
        return (
            device((x + i + NX) % NX, y, z, core) if axis == "x"
            else device(x, (y + i + NY) % NY, z, core) if axis == "y"
            else device(x, y, (z + i + NZ) % NZ, core)
        )

    where = {"x": x, "y": y, "z": z}

    def ring(j):
        axis = "xyxz"[j]
        n = NX if axis == "x" else 8
        o = j // 2

        def own(half, target):
            t = (where[axis] + target + n) % n
            if axis == "x":
                return gpb.at[j, core, t, pl.ds(half * 4, 4)]
            return gpb.at[j, core, pl.ds(half * 2, 2), t]

        def held(half, way, hop):
            return (r1x if axis == "x" else r1a).at[o, half, way, hop]

        def hops(half, way):
            return n // 2 if half == way else n // 2 - 1

        return axis, own, held, hops

    def send(j, hop):
        axis, own, held, hops = ring(j)
        for half in range(2):
            for way in range(2):
                length, sign = hops(half, way), 1 - 2 * way
                if hop >= length:
                    continue
                if hop == 0:
                    source = own(half, sign * length)
                else:
                    source = held(half, way, hop - 1)
                    rcopy(
                        source, source, s_1.at[j, half, way, hop - 1], r_1.at[j, half, way, hop - 1], sibling
                    ).wait_recv()
                    source[...] = source[...] + own(half, sign * (length - hop))[...]
                rcopy(
                    source, held(half, way, hop), s_1.at[j, half, way, hop], r_1.at[j, half, way, hop],
                    along(axis, sign),
                ).start()

    def arrived(j, half):
        axis, own, held, hops = ring(j)
        acc = own(half, 0)[...]
        for way in range(2):
            hop = hops(half, way) - 1
            ref = held(half, way, hop)
            rcopy(ref, ref, s_1.at[j, half, way, hop], r_1.at[j, half, way, hop], sibling).wait_recv()
            acc = acc + ref[...]
        return acc

    for j in order:
        rcopy(gpb.at[j, 1 - core], rc.at[j], s_rc.at[j], r_rc.at[j], sibling).wait_recv()

        def add(i, _, j=j):
            gpb[j, core, i] = gpb[j, core, i] + rc[j, i]
            return 0

        lax.fori_loop(0, NX, add, 0)
        send(j, 0)

    def queries_half(half_at):
        cols = slice(half_at * 512, (half_at + 1) * 512)

        def passages(t, acc):
            at = pl.multiple_of(t * 256, 256)
            w = jnp.transpose(st[pl.ds(at, 256), :]).astype(BF16)
            return acc + mm(w, pall[pl.ds(at, 256), cols])

        def negatives(t, acc):
            at = pl.multiple_of(t * 256, 256)
            w = jnp.transpose(jnp.exp(hs[pl.ds(at, 256), :] - lse)).astype(BF16)
            return acc + mm(w, fn[pl.ds(at, 256), cols])

        acc = lax.fori_loop(0, NP // 256, passages, jnp.zeros((Q, 512), F32))
        acc = lax.fori_loop(0, SLOTS // 256, negatives, acc)
        gq_ref[:, cols] = acc * SCALE

    queries_half(0)
    for j in order:
        send(j, 1)
    queries_half(1)
    for j in (1, 3):
        send(j, 2)
    for j in (0, 2):
        o = j // 2
        a = "yz"[o]
        for half in range(2):
            ax[o, pl.ds(half * 4, 4)] = arrived(j, half)
        for i in range(1, 8):
            rcopy(
                ax.at[o, (where[a] + i) % 8], r2a.at[o, i - 1], s_2.at[j], r_2.at[j], along(a, i)
            ).start()
    for j in (1, 3):
        send(j, 3)
    for j in (1, 3):
        o = j // 2
        for half in range(2):
            aa[o, pl.ds(half * 2, 2)] = arrived(j, half)
        for i in range(1, NX):
            rcopy(
                aa.at[o, (x + i) % NX], r2x.at[o, i - 1], s_2.at[j], r_2.at[j], along("x", i)
            ).start()

    for j in (0, 2, 1, 3):
        o, first_x = j // 2, j % 2 == 0
        a, b = "yz"[o], "zy"[o]
        if first_x:
            rcopy(r2a.at[o], r2a.at[o], s_2.at[j], r_2.at[j], sibling).wait_recv()
            acc = ax[o, where[a]]
            for i in range(7):
                acc = acc + r2a[o, i]
        else:
            rcopy(r2x.at[o], r2x.at[o], s_2.at[j], r_2.at[j], sibling).wait_recv()
            acc = aa[o, x]
            for i in range(NX - 1):
                acc = acc + r2x[o, i]
        for i in range(8):
            a3[j, i] = acc[i * 4:(i + 1) * 4, :]
        for i in range(1, 8):
            rcopy(
                a3.at[j, (where[b] + i) % 8], r3.at[j, i - 1], s_3.at[j], r_3.at[j], along(b, i)
            ).start()

    for j in range(4):
        b = "zy"[j // 2]
        rcopy(r3.at[j], r3.at[j], s_3.at[j], r_3.at[j], sibling).wait_recv()
        acc = a3[j, where[b]]
        for i in range(7):
            acc = acc + r3[j, i]
        gp_ref[:, j * 256:(j + 1) * 256] = acc * SCALE

    def left(ref, sem):
        rcopy(ref, ref, sem, sem, sibling).wait_send()

    left(reqin.at[pl.ds(0, NB - 1)], s_req)
    left(f.at[pl.ds(0, (NB - 1) * SLAB)], s_row)
    left(zbuf.at[pl.ds(0, NZ - 1)], s_ag.at[0])
    left(pall.at[pl.ds(0, 224)], s_ag.at[1])
    for n in range(2):
        left(pall.at[pl.ds(0, 256)], s_ag.at[2 + n])
        left(pall.at[pl.ds(0, 128)], s_ag.at[4 + n])
    left(pall.at[pl.ds(0, 1024)], s_ag.at[6])
    for j in range(4):
        o, first_x = j // 2, j % 2 == 0
        left(rc.at[j], s_rc.at[j])
        _, _, held, hops = ring(j)
        for half in range(2):
            for way in range(2):
                for hop in range(hops(half, way)):
                    left(held(half, way, hop), s_1.at[j, half, way, hop])
        left(r2a.at[o] if first_x else r2x.at[o], s_2.at[j])
        left(r3.at[j], s_3.at[j])


def shards(queries, passages, negatives, neg_ids, positives):
    vmem = pl.BlockSpec(memory_space=pltpu.VMEM)
    dma = pltpu.SemaphoreType.DMA
    req, slots = pl.pallas_call(
        requests,
        out_shape=(
            jax.ShapeDtypeStruct((NB, 1, 128), I32),
            jax.ShapeDtypeStruct((128, Q), I32),
        ),
        in_specs=[vmem],
        out_specs=(vmem, vmem),
    )(neg_ids)
    return pl.pallas_call(
        kernel,
        out_shape=(
            jax.ShapeDtypeStruct((Q, D), F32),
            jax.ShapeDtypeStruct((4, D), F32),
        ),
        in_specs=[vmem] * 6,
        out_specs=(vmem, vmem),
        scratch_shapes=[
            pltpu.VMEM((NB, 1, 128), I32),
            pltpu.SMEM((NB, 1, 128), I32),
            pltpu.VMEM((ROWS, C8, 128), F32),
            pltpu.VMEM((NB * SLAB, 128), BF16),
            pltpu.VMEM((NB * SLAB, 128), BF16),
            pltpu.VMEM((PER * SLAB, 128), F32),
            pltpu.VMEM((SLOTS, D), BF16),
            pltpu.VMEM((NP, Q), F32),
            pltpu.VMEM((SLOTS, Q), F32),
            pltpu.VMEM((32, 128), F32),
            pltpu.VMEM((32, 128), BF16),
            pltpu.VMEM((NZ, 32, 128), BF16),
            pltpu.VMEM((NZ * 32, 128), F32),
            pltpu.VMEM((NP, D), BF16),
            pltpu.VMEM((2, NP, Q), BF16),
            pltpu.VMEM((4, 2, NX, 8, 32, 256), F32),
            pltpu.VMEM((4, NX, 8, 32, 256), F32),
            pltpu.VMEM((2, 2, 2, 2, 4, 32, 256), F32),
            pltpu.VMEM((2, 2, 2, 4, 2, 32, 256), F32),
            pltpu.VMEM((2, 8, 32, 256), F32),
            pltpu.VMEM((2, NX, 32, 256), F32),
            pltpu.VMEM((2, NX - 1, 32, 256), F32),
            pltpu.VMEM((2, 7, 32, 256), F32),
            pltpu.VMEM((4, 8, 4, 256), F32),
            pltpu.VMEM((4, 7, 4, 256), F32),
            dma, dma, dma((7,)), dma, dma((GROUPS,)), dma((7,)),
            dma((4,)), dma((4,)), dma((4, 2, 2, 4)), dma((4, 2, 2, 4)),
            dma((4,)), dma((4,)), dma((4,)), dma((4,)), dma,
        ],
        compiler_params=pltpu.CompilerParams(
            collective_id=0, has_side_effects=True, vmem_limit_bytes=58 * 1024 * 1024
        ),
        cost_estimate=pl.CostEstimate(flops=4 * Q * NP * D * 2, bytes_accessed=1 << 24, transcendentals=0),
    )(req, slots, positives.reshape(1, Q), passages, queries, negatives)


def solution(mesh):
    rows = P(("blk", "grp"), None)
    return jax.shard_map(
        shards,
        mesh=mesh,
        in_specs=(rows, rows, rows, rows, P(("blk", "grp"))),
        out_specs=(rows, rows),
        check_vma=False,
    )
```

```python
import functools
import math

import jax
import jax.numpy as jnp
from jax import lax
from jax.experimental import pallas as pl
from jax.experimental.pallas import tpu as pltpu
from jax.sharding import PartitionSpec as P

MESH = pl.DeviceIdType.MESH
F32, BF16, I32 = jnp.float32, jnp.bfloat16, jnp.int32

NX, NY, NZ, NYL = 4, 8, 8, 4
NB = 128
MUL, INV = 37, 45
CAP = 10
Q, D, HARD, ROWS = 128, 1024, 7, 896
C8 = D // 128
SLAB = CAP * C8
GROUPS = 8
PER = NB // GROUPS
SLOTS = NB * CAP
NP = 2048
SCALE = 3.0 / math.sqrt(D)
NEG = -1e30


def device(x, y, z, core):
    return (((y % NYL) * NX + x) * NZ + z, (y // NYL) * 2 + core)


def rcopy(src, dst, send, recv, dev):
    return pltpu.make_async_remote_copy(
        src_ref=src, dst_ref=dst, send_sem=send, recv_sem=recv, device_id=dev, device_id_type=MESH
    )


def nt(left, right):
    return lax.dot_general(left, right, (((1,), (1,)), ((), ())), preferred_element_type=F32)


def mm(left, right):
    return lax.dot_general(left, right, (((1,), (0,)), ((), ())), preferred_element_type=F32)


def iota(shape, dim):
    return lax.broadcasted_iota(I32, shape, dim)


def requests(ids_ref, req, slots):
    mb = lax.axis_index("blk")
    sub = iota((128, Q), 0)
    before = (iota((Q, Q), 0) < iota((Q, Q), 1)).astype(F32).astype(BF16)
    base = jnp.zeros((NB, 1), F32)
    want_hi = jnp.zeros((NB, 128), F32)
    want_lo = jnp.zeros((NB, 128), F32)
    slots[...] = jnp.full((8, Q), -1, I32)
    for k in range(HARD):
        ids = ids_ref[k:k + 1, :]
        dev = jnp.floor((ids.astype(F32) + 0.5) * (1.0 / ROWS)).astype(I32)
        row = ids - dev * ROWS
        off = (dev >> 2) ^ mb
        kz, kxy = off & (NZ - 1), off >> 3
        step = (off * INV) & (NB - 1)
        hot = (sub == kz * 16 + kxy).astype(F32)
        hot16 = hot.astype(BF16)
        rank = jnp.sum(hot * (mm(hot16, before) + base), axis=0, keepdims=True).astype(I32)
        base = base + jnp.sum(hot, axis=1, keepdims=True)
        slots[k:k + 1, :] = step * CAP + rank
        at_lane = (sub == kz * 16 + rank).astype(F32)
        want_hi = want_hi + nt(hot16, (at_lane * (row >> 3).astype(F32)).astype(BF16))
        want_lo = want_lo + nt(hot16, (at_lane * (row & 7).astype(F32)).astype(BF16))
    req[...] = (want_hi * 8.0 + want_lo).astype(I32).reshape(NZ, 16, 1, 128)


def scaled(gq_in, gp_in, gq_ref, gp_ref):
    gq_ref[...] = gq_in[...] * SCALE
    gp_ref[...] = gp_in[...] * SCALE


def kernel(
    req, slots, pos_ref, pas_ref, q_ref, neg_ref,
    gq_ref, gp_ref,
    asked, passed, reqin, idsm, tab, g, f, fs, fn, st, hs, pst, pmine, zbuf, zf, pall,
    wt, gpb, rc, r1x, r1a, ax, aa, r2x, r2a, a3, r3,
    s_req, s_pass, s_y, s_row, s_ag, r_req, r_pass, r_y, r_row, r_ag, s_rc, r_rc, s_1, r_1, s_2, r_2, s_3, r_3, s_loc,
):
    mb = lax.axis_index("blk")
    mg = lax.axis_index("grp")
    yl, x, z = mb // (NX * NZ), (mb // NZ) % NX, mb % NZ
    yh, core = mg // 2, mg % 2
    y = yh * NYL + yl

    def partner(step):
        return (mb ^ ((step * MUL) & (NB - 1)), mg)

    sibling = device(x, y, z, 1 - core)

    barrier = pltpu.get_barrier_semaphore()

    def greet(dev):
        pl.semaphore_signal(barrier, inc=1, device_id=dev, device_id_type=MESH)

    for i in range(1, NZ):
        greet((mb ^ i, mg))
    for n in range(1, 16):
        greet((mb ^ (n * NZ), mg))
    for i in range(NYL):
        greet(device(x, (1 - yh) * NYL + i, z, core))
    greet(sibling)

    for c in range(C8):
        pst[pl.ds(c, 4, stride=C8), :] = pas_ref[:, c * 128:(c + 1) * 128].astype(F32)
    own = pst[...].astype(BF16)
    pmine[...] = own
    zbuf[z] = own

    pl.semaphore_wait(barrier, NZ - 1 + 15 + NYL + 1)

    for i in range(1, NZ):
        rcopy(req.at[i], asked.at[i], s_req, r_req, (mb ^ i, mg)).start()
    asked[0] = req[0]

    for i in range(1, NZ):
        to = device(x, y, (z + i) % NZ, core)
        rcopy(pmine, zbuf.at[z], s_ag.at[0], r_ag.at[0], to).start()

    rcopy(asked.at[pl.ds(0, NZ - 1)], asked.at[pl.ds(0, NZ - 1)], s_req, r_req, sibling).wait_recv()
    total = asked[0]
    for i in range(1, NZ):
        total = total + asked[i]
    passed[...] = total
    for n in range(1, 16):
        rcopy(passed.at[n], reqin.at[n], s_pass, r_pass, (mb ^ (n * NZ), mg)).start()
    reqin[0] = passed[0]

    flat = tab.reshape(ROWS * C8, 128)
    for t in range(ROWS // 128):
        for c in range(C8):
            part = neg_ref[t * 128:(t + 1) * 128, c * 128:(c + 1) * 128].astype(F32)
            flat[pl.ds(t * 1024 + c, 128, stride=C8), :] = part

    rcopy(zbuf.at[pl.ds(0, NZ - 1)], zbuf.at[pl.ds(0, NZ - 1)], s_ag.at[0], r_ag.at[0], sibling).wait_recv()
    zf[...] = zbuf[...].reshape(NZ * 32, 128).astype(F32)
    mine = pl.multiple_of(((core * NX + x) * NY + y) * 32, 32)
    for c in range(C8):
        pall[pl.ds(mine, 32), c * 128:(c + 1) * 128] = zf[pl.ds(c, 32, stride=C8), :].astype(BF16)

    def along_y(hop):
        for n in range(2):
            sign = 1 - 2 * n
            rows = 16 if hop == 3 else 32
            at = ((core * NX + x) * NY + (y + NY - sign * hop) % NY) * 32 + (16 * n if hop == 3 else 0)
            block = pall.at[pl.ds(pl.multiple_of(at, 16), rows)]
            if hop:
                came = pall.at[pl.ds(0, 32)]
                rcopy(came, came, s_y.at[n, hop - 1], r_y.at[n, hop - 1], sibling).wait_recv()
            to = device(x, (y + NY + sign) % NY, z, core)
            rcopy(block, block, s_y.at[n, hop], r_y.at[n, hop], to).start()

    along_y(0)

    rcopy(reqin.at[pl.ds(0, 15)], reqin.at[pl.ds(0, 15)], s_pass, r_pass, sibling).wait_recv()
    local = pltpu.make_async_copy(reqin, idsm, s_loc)
    local.start()
    local.wait()

    def pick(step, dst):
        at = pl.multiple_of(step * SLAB, 16)
        k = (step * MUL) % NB
        n, lane = k // NZ, (k % NZ) * 16
        for j in range(CAP // 2):
            pair = jnp.concatenate([tab[idsm[n, 0, lane + 2 * j]], tab[idsm[n, 0, lane + 2 * j + 1]]], axis=0)
            dst[pl.ds(at + 16 * j, 16), :] = pair.astype(BF16)

    def answer(step, _):
        pick(step, g)
        at = pl.multiple_of(step * SLAB, 16)
        rcopy(
            g.at[pl.ds(at, SLAB)], f.at[pl.ds(at, SLAB)], s_row, r_row.at[step // PER], partner(step)
        ).start()
        return 0

    lax.fori_loop(1, 16, answer, 0)
    along_y(1)
    lax.fori_loop(16, 32, answer, 0)
    along_y(2)
    lax.fori_loop(32, 48, answer, 0)
    along_y(3)
    lax.fori_loop(48, NB, answer, 0)
    pick(0, f)

    for n in range(2):
        came = pall.at[pl.ds(0, 16)]
        rcopy(came, came, s_y.at[n, 3], r_y.at[n, 3], sibling).wait_recv()
    right, left_x = device((x + 1) % NX, y, z, core), device((x + NX - 1) % NX, y, z, core)

    def slab(at, rows, extra=0):
        return pall.at[pl.ds(pl.multiple_of((core * NX + at) * 256 + extra, 128), rows)]

    for n, to in ((0, right), (1, left_x)):
        rcopy(slab(x, 256), slab(x, 256), s_ag.at[2 + n], r_ag.at[2 + n], to).start()
    for n, to in ((0, right), (1, left_x)):
        came = (x + NX - 1) % NX if n == 0 else (x + 1) % NX
        rcopy(slab(came, 256), slab(came, 256), s_ag.at[2 + n], r_ag.at[2 + n], to).wait_recv()
        part = slab(came, 128, 128 * n)
        rcopy(part, part, s_ag.at[4 + n], r_ag.at[4 + n], to).start()
    for n in range(2):
        part = slab((x + 2) % NX, 128, 128 * n)
        rcopy(part, part, s_ag.at[4 + n], r_ag.at[4 + n], sibling).wait_recv()
    half = pall.at[pl.ds(pl.multiple_of(core * 1024, 1024), 1024)]
    rcopy(half, half, s_ag.at[6], r_ag.at[6], sibling).start()
    rcopy(half, half, s_ag.at[6], r_ag.at[6], sibling).wait_recv()

    def score(t, top):
        at = pl.multiple_of(t * 256, 256)
        part = nt(pall[pl.ds(at, 256), :], q_ref[...]) * SCALE
        st[pl.ds(at, 256), :] = part
        return jnp.maximum(top, jnp.max(part, axis=0, keepdims=True))

    pool_top = lax.fori_loop(0, NP // 256, score, jnp.full((1, Q), NEG, F32))

    def raise_(t, total):
        at = pl.multiple_of(t * 256, 256)
        part = jnp.exp(st[pl.ds(at, 256), :] - pool_top)
        st[pl.ds(at, 256), :] = part
        return total + jnp.sum(part, axis=0, keepdims=True)

    pool_total = lax.fori_loop(0, NP // 256, raise_, jnp.zeros((1, Q), F32))
    top = pool_top

    def hard(group, top):
        at = pl.multiple_of(group * PER * SLAB, PER * SLAB)
        row0 = pl.multiple_of(group * PER * CAP, PER * CAP)
        fs[...] = f[pl.ds(at, PER * SLAB), :].astype(F32)
        for c in range(C8):
            fn[pl.ds(row0, PER * CAP), c * 128:(c + 1) * 128] = fs[
                pl.ds(c, PER * CAP, stride=C8), :
            ].astype(BF16)
        part = nt(fn[pl.ds(row0, PER * CAP), :], q_ref[...]) * SCALE
        number = iota((PER * CAP, Q), 0) + row0
        taken = number == slots[0:1, :]
        for k in range(1, HARD):
            taken = taken | (number == slots[k:k + 1, :])
        part = jnp.where(taken, part, NEG)
        hs[pl.ds(row0, PER * CAP), :] = part
        return jnp.maximum(top, jnp.max(part, axis=0, keepdims=True))

    for group in range(GROUPS):
        n = PER - (1 if group == 0 else 0)
        ref = f.at[pl.ds(0, n * SLAB)]
        rcopy(ref, ref, s_row, r_row.at[group], sibling).wait_recv()
        top = hard(group, top)

    total = pool_total * jnp.exp(pool_top - top) + jnp.sum(jnp.exp(hs[...] - top), axis=0, keepdims=True)
    lse = top + jnp.log(total)
    factor = jnp.exp(pool_top - lse)

    p = pos_ref[...]
    answer_slot = (
        (((p >> 2) & 1) << 10)
        | (((p >> 7) & 3) << 8)
        | (((p >> 3) & 1) << 7)
        | (((p >> 9) & 3) << 5)
        | (((p >> 4) & 7) << 2)
        | (p & 3)
    )
    there = iota((256, 256), 0)
    source = (((there >> 2) & 7) << 5) | ((there >> 5) << 2) | (there & 3)
    swap = (iota((256, 256), 1) == source).astype(F32).astype(BF16)

    def weigh(side):
        def one(i, _):
            at = pl.multiple_of(side * 1024 + i * 256, 256)
            hit = (iota((256, Q), 0) + at == answer_slot).astype(F32)
            w = st[pl.ds(at, 256), :] * factor - hit
            st[pl.ds(at, 256), :] = w
            w = w.astype(BF16)
            wt[0, pl.ds(at, 256), :] = w
            wt[1, pl.ds(at, 256), :] = mm(swap, w).astype(BF16)
            return 0

        lax.fori_loop(0, NX, one, 0)

    def grads(j, side):
        def one(i, _):
            at = pl.multiple_of(side * 1024 + i * 256, 256)
            part = mm(wt[j // 2, pl.ds(at, 256), :], q_ref[:, j * 256:(j + 1) * 256])
            gpb[j, side, i] = part.reshape(8, 32, 256)
            return 0

        lax.fori_loop(0, NX, one, 0)

    order = (1, 3, 0, 2)
    weigh(1 - core)
    for j in order:
        grads(j, 1 - core)
        rcopy(gpb.at[j, 1 - core], rc.at[j], s_rc.at[j], r_rc.at[j], sibling).start()
    weigh(core)
    for j in order:
        grads(j, core)

    def along(axis, i):
        return (
            device((x + i + NX) % NX, y, z, core) if axis == "x"
            else device(x, (y + i + NY) % NY, z, core) if axis == "y"
            else device(x, y, (z + i + NZ) % NZ, core)
        )

    where = {"x": x, "y": y, "z": z}

    def ring(j):
        axis = "xyxz"[j]
        n = NX if axis == "x" else 8
        o = j // 2

        def own(half, target):
            t = (where[axis] + target + n) % n
            if axis == "x":
                return gpb.at[j, core, t, pl.ds(half * 4, 4)]
            return gpb.at[j, core, pl.ds(half * 2, 2), t]

        def held(half, way, hop):
            return (r1x if axis == "x" else r1a).at[o, half, way, hop]

        def hops(half, way):
            return n // 2 if half == way else n // 2 - 1

        return axis, own, held, hops

    def send(j, hop):
        axis, own, held, hops = ring(j)
        for half in range(2):
            for way in range(2):
                length, sign = hops(half, way), 1 - 2 * way
                if hop >= length:
                    continue
                if hop == 0:
                    source = own(half, sign * length)
                else:
                    source = held(half, way, hop - 1)
                    rcopy(
                        source, source, s_1.at[j, half, way, hop - 1], r_1.at[j, half, way, hop - 1], sibling
                    ).wait_recv()
                    source[...] = source[...] + own(half, sign * (length - hop))[...]
                rcopy(
                    source, held(half, way, hop), s_1.at[j, half, way, hop], r_1.at[j, half, way, hop],
                    along(axis, sign),
                ).start()

    def arrived(j, half):
        axis, own, held, hops = ring(j)
        acc = own(half, 0)[...]
        for way in range(2):
            hop = hops(half, way) - 1
            ref = held(half, way, hop)
            rcopy(ref, ref, s_1.at[j, half, way, hop], r_1.at[j, half, way, hop], sibling).wait_recv()
            acc = acc + ref[...]
        return acc

    for j in order:
        rcopy(gpb.at[j, 1 - core], rc.at[j], s_rc.at[j], r_rc.at[j], sibling).wait_recv()

        def add(i, _, j=j):
            gpb[j, core, i] = gpb[j, core, i] + rc[j, i]
            return 0

        lax.fori_loop(0, NX, add, 0)
        send(j, 0)

    def queries_half(half_at):
        cols = slice(half_at * 512, (half_at + 1) * 512)

        def passages(t, acc):
            at = pl.multiple_of(t * 256, 256)
            w = jnp.transpose(st[pl.ds(at, 256), :]).astype(BF16)
            return acc + mm(w, pall[pl.ds(at, 256), cols])

        def negatives(t, acc):
            at = pl.multiple_of(t * 256, 256)
            w = jnp.transpose(jnp.exp(hs[pl.ds(at, 256), :] - lse)).astype(BF16)
            return acc + mm(w, fn[pl.ds(at, 256), cols])

        acc = lax.fori_loop(0, NP // 256, passages, jnp.zeros((Q, 512), F32))
        acc = lax.fori_loop(0, SLOTS // 256, negatives, acc)
        gq_ref[:, cols] = acc

    queries_half(0)
    for j in order:
        send(j, 1)
    queries_half(1)
    for j in (1, 3):
        send(j, 2)
    for j in (0, 2):
        o = j // 2
        a = "yz"[o]
        for half in range(2):
            ax[o, pl.ds(half * 4, 4)] = arrived(j, half)
        for i in range(1, 8):
            rcopy(
                ax.at[o, (where[a] + i) % 8], r2a.at[o, i - 1], s_2.at[j], r_2.at[j], along(a, i)
            ).start()
    for j in (1, 3):
        send(j, 3)
    for j in (1, 3):
        o = j // 2
        for half in range(2):
            aa[o, pl.ds(half * 2, 2)] = arrived(j, half)
        for i in range(1, NX):
            rcopy(
                aa.at[o, (x + i) % NX], r2x.at[o, i - 1], s_2.at[j], r_2.at[j], along("x", i)
            ).start()

    for j in (0, 2, 1, 3):
        o, first_x = j // 2, j % 2 == 0
        a, b = "yz"[o], "zy"[o]
        if first_x:
            rcopy(r2a.at[o], r2a.at[o], s_2.at[j], r_2.at[j], sibling).wait_recv()
            acc = ax[o, where[a]]
            for i in range(7):
                acc = acc + r2a[o, i]
        else:
            rcopy(r2x.at[o], r2x.at[o], s_2.at[j], r_2.at[j], sibling).wait_recv()
            acc = aa[o, x]
            for i in range(NX - 1):
                acc = acc + r2x[o, i]
        for i in range(8):
            a3[j, i] = acc[i * 4:(i + 1) * 4, :]
        for i in range(1, 8):
            rcopy(
                a3.at[j, (where[b] + i) % 8], r3.at[j, i - 1], s_3.at[j], r_3.at[j], along(b, i)
            ).start()

    for j in range(4):
        b = "zy"[j // 2]
        rcopy(r3.at[j], r3.at[j], s_3.at[j], r_3.at[j], sibling).wait_recv()
        acc = a3[j, where[b]]
        for i in range(7):
            acc = acc + r3[j, i]
        gp_ref[:, j * 256:(j + 1) * 256] = acc

    def left(ref, sem):
        rcopy(ref, ref, sem, sem, sibling).wait_send()

    left(asked.at[pl.ds(0, NZ - 1)], s_req)
    left(reqin.at[pl.ds(0, 15)], s_pass)
    left(f.at[pl.ds(0, (NB - 1) * SLAB)], s_row)
    left(zbuf.at[pl.ds(0, NZ - 1)], s_ag.at[0])
    for n in range(2):
        for hop in range(4):
            left(pall.at[pl.ds(0, 16 if hop == 3 else 32)], s_y.at[n, hop])
    for n in range(2):
        left(pall.at[pl.ds(0, 256)], s_ag.at[2 + n])
        left(pall.at[pl.ds(0, 128)], s_ag.at[4 + n])
    left(pall.at[pl.ds(0, 1024)], s_ag.at[6])
    for j in range(4):
        o, first_x = j // 2, j % 2 == 0
        left(rc.at[j], s_rc.at[j])
        _, _, held, hops = ring(j)
        for half in range(2):
            for way in range(2):
                for hop in range(hops(half, way)):
                    left(held(half, way, hop), s_1.at[j, half, way, hop])
        left(r2a.at[o] if first_x else r2x.at[o], s_2.at[j])
        left(r3.at[j], s_3.at[j])


def shards(queries, passages, negatives, neg_ids, positives):
    vmem = pl.BlockSpec(memory_space=pltpu.VMEM)
    dma = pltpu.SemaphoreType.DMA
    req, slots = pl.pallas_call(
        requests,
        out_shape=(
            jax.ShapeDtypeStruct((NZ, 16, 1, 128), I32),
            jax.ShapeDtypeStruct((8, Q), I32),
        ),
        in_specs=[vmem],
        out_specs=(vmem, vmem),
    )(neg_ids.T)
    sums = pl.pallas_call(
        kernel,
        out_shape=(
            jax.ShapeDtypeStruct((Q, D), F32),
            jax.ShapeDtypeStruct((4, D), F32),
        ),
        in_specs=[vmem] * 6,
        out_specs=(vmem, vmem),
        scratch_shapes=[
            pltpu.VMEM((NZ, 16, 1, 128), I32),
            pltpu.VMEM((16, 1, 128), I32),
            pltpu.VMEM((16, 1, 128), I32),
            pltpu.SMEM((16, 1, 128), I32),
            pltpu.VMEM((ROWS, C8, 128), F32),
            pltpu.VMEM((NB * SLAB, 128), BF16),
            pltpu.VMEM((NB * SLAB, 128), BF16),
            pltpu.VMEM((PER * SLAB, 128), F32),
            pltpu.VMEM((SLOTS, D), BF16),
            pltpu.VMEM((NP, Q), F32),
            pltpu.VMEM((SLOTS, Q), F32),
            pltpu.VMEM((32, 128), F32),
            pltpu.VMEM((32, 128), BF16),
            pltpu.VMEM((NZ, 32, 128), BF16),
            pltpu.VMEM((NZ * 32, 128), F32),
            pltpu.VMEM((NP, D), BF16),
            pltpu.VMEM((2, NP, Q), BF16),
            pltpu.VMEM((4, 2, NX, 8, 32, 256), F32),
            pltpu.VMEM((4, NX, 8, 32, 256), F32),
            pltpu.VMEM((2, 2, 2, 2, 4, 32, 256), F32),
            pltpu.VMEM((2, 2, 2, 4, 2, 32, 256), F32),
            pltpu.VMEM((2, 8, 32, 256), F32),
            pltpu.VMEM((2, NX, 32, 256), F32),
            pltpu.VMEM((2, NX - 1, 32, 256), F32),
            pltpu.VMEM((2, 7, 32, 256), F32),
            pltpu.VMEM((4, 8, 4, 256), F32),
            pltpu.VMEM((4, 7, 4, 256), F32),
            dma, dma, dma((2, 4)), dma, dma((7,)), dma, dma, dma((2, 4)), dma((GROUPS,)), dma((7,)),
            dma((4,)), dma((4,)), dma((4, 2, 2, 4)), dma((4, 2, 2, 4)),
            dma((4,)), dma((4,)), dma((4,)), dma((4,)), dma,
        ],
        compiler_params=pltpu.CompilerParams(
            collective_id=0, has_side_effects=True, vmem_limit_bytes=58 * 1024 * 1024
        ),
        cost_estimate=pl.CostEstimate(flops=4 * Q * NP * D * 2, bytes_accessed=1 << 24, transcendentals=0),
    )(req, slots, positives.reshape(1, Q), passages, queries, negatives)
    return pl.pallas_call(
        scaled,
        out_shape=(
            jax.ShapeDtypeStruct((Q, D), F32),
            jax.ShapeDtypeStruct((4, D), F32),
        ),
        in_specs=[vmem] * 2,
        out_specs=(vmem, vmem),
    )(*sums)


def solution(mesh):
    rows = P(("blk", "grp"), None)
    return jax.shard_map(
        shards,
        mesh=mesh,
        in_specs=(rows, rows, rows, rows, P(("blk", "grp"))),
        out_specs=(rows, rows),
        check_vma=False,
    )
```

```python
import functools
import math

import jax
import jax.numpy as jnp
from jax import lax
from jax.experimental import pallas as pl
from jax.experimental.pallas import tpu as pltpu
from jax.sharding import PartitionSpec as P

MESH = pl.DeviceIdType.MESH
F32, BF16, I32 = jnp.float32, jnp.bfloat16, jnp.int32

NX, NY, NZ, NYL = 4, 8, 8, 4
NB = 128
MUL, INV = 37, 45
CAP = 10
Q, D, HARD, ROWS = 128, 1024, 7, 896
C8 = D // 128
SLAB = CAP * C8
GROUPS = 8
PER = NB // GROUPS
CHUNKS = 16
STEPS = NB // CHUNKS
SLOTS = NB * CAP
NP = 2048
SCALE = 3.0 / math.sqrt(D)
NEG = -1e30


def device(x, y, z, core):
    return (((y % NYL) * NX + x) * NZ + z, (y // NYL) * 2 + core)


def rcopy(src, dst, send, recv, dev):
    return pltpu.make_async_remote_copy(
        src_ref=src, dst_ref=dst, send_sem=send, recv_sem=recv, device_id=dev, device_id_type=MESH
    )


def nt(left, right):
    return lax.dot_general(left, right, (((1,), (1,)), ((), ())), preferred_element_type=F32)


def mm(left, right):
    return lax.dot_general(left, right, (((1,), (0,)), ((), ())), preferred_element_type=F32)


def iota(shape, dim):
    return lax.broadcasted_iota(I32, shape, dim)


def requests(ids_ref, req, slots):
    mb = lax.axis_index("blk")
    sub = iota((128, Q), 0)
    before = (iota((Q, Q), 0) < iota((Q, Q), 1)).astype(F32).astype(BF16)
    base = jnp.zeros((NB, 1), F32)
    want_hi = jnp.zeros((NB, 128), F32)
    want_lo = jnp.zeros((NB, 128), F32)
    slots[...] = jnp.full((8, Q), -1, I32)
    for k in range(HARD):
        ids = ids_ref[k:k + 1, :]
        dev = jnp.floor((ids.astype(F32) + 0.5) * (1.0 / ROWS)).astype(I32)
        row = ids - dev * ROWS
        off = (dev >> 2) ^ mb
        kz, kxy = off & (NZ - 1), off >> 3
        step = (off * INV) & (NB - 1)
        hot = (sub == kz * 16 + kxy).astype(F32)
        hot16 = hot.astype(BF16)
        rank = jnp.sum(hot * (mm(hot16, before) + base), axis=0, keepdims=True).astype(I32)
        base = base + jnp.sum(hot, axis=1, keepdims=True)
        slots[k:k + 1, :] = step * CAP + rank
        at_lane = (sub == kz * 16 + rank).astype(F32)
        want_hi = want_hi + nt(hot16, (at_lane * (row >> 3).astype(F32)).astype(BF16))
        want_lo = want_lo + nt(hot16, (at_lane * (row & 7).astype(F32)).astype(BF16))
    req[...] = (want_hi * 8.0 + want_lo).astype(I32).reshape(NZ, 16, 1, 128)


def scaled(gq_in, gp_in, gq_ref, gp_ref):
    gq_ref[...] = gq_in[...] * SCALE
    gp_ref[...] = gp_in[...] * SCALE


def kernel(
    req, slots, pos_ref, pas_ref, q_ref, neg_ref,
    gq_ref, gp_ref,
    asked, passed, reqin, idsm, tab, g, f, fs, fn, st, hs, pst, pmine, zbuf, zf, pall,
    wt, gpb, rc, r1x, r1a, ax, aa, r2x, r2a, a3, r3,
    s_req, s_pass, s_y, s_row, s_ag, r_req, r_pass, r_y, r_row, r_ag, s_rc, r_rc, s_1, r_1, s_2, r_2, s_3, r_3, s_loc,
):
    mb = lax.axis_index("blk")
    mg = lax.axis_index("grp")
    yl, x, z = mb // (NX * NZ), (mb // NZ) % NX, mb % NZ
    yh, core = mg // 2, mg % 2
    y = yh * NYL + yl

    def partner(step):
        return (mb ^ ((step * MUL) & (NB - 1)), mg)

    sibling = device(x, y, z, 1 - core)

    barrier = pltpu.get_barrier_semaphore()

    def greet(dev):
        pl.semaphore_signal(barrier, inc=1, device_id=dev, device_id_type=MESH)

    for i in range(1, NZ):
        greet((mb ^ i, mg))
    for n in range(1, 16):
        greet((mb ^ (n * NZ), mg))
    for i in range(NYL):
        greet(device(x, (1 - yh) * NYL + i, z, core))
    greet(sibling)

    for c in range(C8):
        pst[pl.ds(c, 4, stride=C8), :] = pas_ref[:, c * 128:(c + 1) * 128].astype(F32)
    own = pst[...].astype(BF16)
    pmine[...] = own
    zbuf[z] = own

    pl.semaphore_wait(barrier, NZ - 1 + 15 + NYL + 1)

    for i in range(1, NZ):
        rcopy(req.at[i], asked.at[i], s_req, r_req, (mb ^ i, mg)).start()
    asked[0] = req[0]

    for i in range(1, NZ):
        to = device(x, y, (z + i) % NZ, core)
        rcopy(pmine, zbuf.at[z], s_ag.at[0], r_ag.at[0], to).start()

    rcopy(asked.at[pl.ds(0, NZ - 1)], asked.at[pl.ds(0, NZ - 1)], s_req, r_req, sibling).wait_recv()
    total = asked[0]
    for i in range(1, NZ):
        total = total + asked[i]
    passed[...] = total
    for n in range(1, 16):
        rcopy(passed.at[n], reqin.at[n], s_pass, r_pass, (mb ^ (n * NZ), mg)).start()
    reqin[0] = passed[0]

    flat = tab.reshape(ROWS * C8, 128)
    for t in range(ROWS // 128):
        for c in range(C8):
            part = neg_ref[t * 128:(t + 1) * 128, c * 128:(c + 1) * 128].astype(F32)
            flat[pl.ds(t * 1024 + c, 128, stride=C8), :] = part

    rcopy(zbuf.at[pl.ds(0, NZ - 1)], zbuf.at[pl.ds(0, NZ - 1)], s_ag.at[0], r_ag.at[0], sibling).wait_recv()
    zf[...] = zbuf[...].reshape(NZ * 32, 128).astype(F32)
    mine = pl.multiple_of(((core * NX + x) * NY + y) * 32, 32)
    for c in range(C8):
        pall[pl.ds(mine, 32), c * 128:(c + 1) * 128] = zf[pl.ds(c, 32, stride=C8), :].astype(BF16)

    def along_y(hop):
        for n in range(2):
            sign = 1 - 2 * n
            rows = 16 if hop == 3 else 32
            at = ((core * NX + x) * NY + (y + NY - sign * hop) % NY) * 32 + (16 * n if hop == 3 else 0)
            block = pall.at[pl.ds(pl.multiple_of(at, 16), rows)]
            if hop:
                came = pall.at[pl.ds(0, 32)]
                rcopy(came, came, s_y.at[n, hop - 1], r_y.at[n, hop - 1], sibling).wait_recv()
            to = device(x, (y + NY + sign) % NY, z, core)
            rcopy(block, block, s_y.at[n, hop], r_y.at[n, hop], to).start()

    along_y(0)

    rcopy(reqin.at[pl.ds(0, 15)], reqin.at[pl.ds(0, 15)], s_pass, r_pass, sibling).wait_recv()
    local = pltpu.make_async_copy(reqin, idsm, s_loc)
    local.start()
    local.wait()

    def pick(step, dst):
        at = pl.multiple_of(step * SLAB, 16)
        k = (step * MUL) % NB
        n, lane = k // NZ, (k % NZ) * 16
        for j in range(CAP // 2):
            pair = jnp.concatenate([tab[idsm[n, 0, lane + 2 * j]], tab[idsm[n, 0, lane + 2 * j + 1]]], axis=0)
            dst[pl.ds(at + 16 * j, 16), :] = pair.astype(BF16)

    def answer(step, _):
        pick(step, g)
        at = pl.multiple_of(step * SLAB, 16)
        rcopy(
            g.at[pl.ds(at, SLAB)], f.at[pl.ds(at, SLAB)], s_row.at[step // STEPS], r_row.at[step // PER], partner(step)
        ).start()
        return 0

    def gone(chunk):
        ref = f.at[pl.ds(0, (STEPS - (1 if chunk == 0 else 0)) * SLAB)]
        rcopy(ref, ref, s_row.at[chunk], s_row.at[chunk], sibling).wait_send()

    def answers(chunk):
        lax.fori_loop(max(1, chunk * STEPS), (chunk + 1) * STEPS, answer, 0)
        if chunk >= 2:
            gone(chunk - 2)

    right, left_x = device((x + 1) % NX, y, z, core), device((x + NX - 1) % NX, y, z, core)

    def slab(at, rows, extra=0):
        return pall.at[pl.ds(pl.multiple_of((core * NX + at) * 256 + extra, 128), rows)]

    def along_x(hop):
        for n, to in ((0, right), (1, left_x)):
            if hop == 0:
                came = pall.at[pl.ds(0, 16)]
                rcopy(came, came, s_y.at[n, 3], r_y.at[n, 3], sibling).wait_recv()
        for n, to in ((0, right), (1, left_x)):
            if hop == 0:
                rcopy(slab(x, 256), slab(x, 256), s_ag.at[2 + n], r_ag.at[2 + n], to).start()
            else:
                came = (x + NX - 1) % NX if n == 0 else (x + 1) % NX
                rcopy(slab(came, 256), slab(came, 256), s_ag.at[2 + n], r_ag.at[2 + n], to).wait_recv()
                part = slab(came, 128, 128 * n)
                rcopy(part, part, s_ag.at[4 + n], r_ag.at[4 + n], to).start()

    half = pall.at[pl.ds(pl.multiple_of(core * 1024, 1024), 1024)]

    def across():
        for n in range(2):
            part = slab((x + 2) % NX, 128, 128 * n)
            rcopy(part, part, s_ag.at[4 + n], r_ag.at[4 + n], sibling).wait_recv()
        rcopy(half, half, s_ag.at[6], r_ag.at[6], sibling).start()

    def score(t, top):
        at = pl.multiple_of(t * 256, 256)
        part = nt(pall[pl.ds(at, 256), :], q_ref[...]) * SCALE
        st[pl.ds(at, 256), :] = part
        return jnp.maximum(top, jnp.max(part, axis=0, keepdims=True))

    def raise_(t, carry):
        pool_top, total = carry
        at = pl.multiple_of(t * 256, 256)
        part = jnp.exp(st[pl.ds(at, 256), :] - pool_top)
        st[pl.ds(at, 256), :] = part
        return pool_top, total + jnp.sum(part, axis=0, keepdims=True)

    def pool():
        rcopy(half, half, s_ag.at[6], r_ag.at[6], sibling).wait_recv()
        pool_top = lax.fori_loop(0, NP // 256, score, jnp.full((1, Q), NEG, F32))
        return lax.fori_loop(0, NP // 256, raise_, (pool_top, jnp.zeros((1, Q), F32)))

    def hard(group, top):
        at = pl.multiple_of(group * PER * SLAB, PER * SLAB)
        row0 = pl.multiple_of(group * PER * CAP, PER * CAP)
        fs[...] = f[pl.ds(at, PER * SLAB), :].astype(F32)
        for c in range(C8):
            fn[pl.ds(row0, PER * CAP), c * 128:(c + 1) * 128] = fs[
                pl.ds(c, PER * CAP, stride=C8), :
            ].astype(BF16)
        part = nt(fn[pl.ds(row0, PER * CAP), :], q_ref[...]) * SCALE
        number = iota((PER * CAP, Q), 0) + row0
        taken = number == slots[0:1, :]
        for k in range(1, HARD):
            taken = taken | (number == slots[k:k + 1, :])
        part = jnp.where(taken, part, NEG)
        hs[pl.ds(row0, PER * CAP), :] = part
        return jnp.maximum(top, jnp.max(part, axis=0, keepdims=True))

    def group_in(group, top):
        n = PER - (1 if group == 0 else 0)
        ref = f.at[pl.ds(0, n * SLAB)]
        rcopy(ref, ref, s_pass, r_row.at[group], sibling).wait_recv()
        return hard(group, top)

    hard_top = jnp.full((1, Q), NEG, F32)
    along_y(1)
    for chunk in range(CHUNKS):
        answers(chunk)
        if chunk == 0:
            pick(0, f)
            along_y(2)
        elif chunk == 1:
            along_y(3)
        elif chunk == 2:
            along_x(0)
        elif chunk == 5:
            along_x(1)
        elif chunk == 7:
            across()
        elif chunk == 10:
            pool_top, pool_total = pool()
        if chunk >= 5 and chunk % 2 == 1:
            hard_top = group_in((chunk - 5) // 2, hard_top)
    for group in range((CHUNKS - 4) // 2, GROUPS):
        hard_top = group_in(group, hard_top)
    top = jnp.maximum(pool_top, hard_top)

    total = pool_total * jnp.exp(pool_top - top) + jnp.sum(jnp.exp(hs[...] - top), axis=0, keepdims=True)
    lse = top + jnp.log(total)
    factor = jnp.exp(pool_top - lse)

    p = pos_ref[...]
    answer_slot = (
        (((p >> 2) & 1) << 10)
        | (((p >> 7) & 3) << 8)
        | (((p >> 3) & 1) << 7)
        | (((p >> 9) & 3) << 5)
        | (((p >> 4) & 7) << 2)
        | (p & 3)
    )
    there = iota((256, 256), 0)
    source = (((there >> 2) & 7) << 5) | ((there >> 5) << 2) | (there & 3)
    swap = (iota((256, 256), 1) == source).astype(F32).astype(BF16)

    def weigh(side):
        def one(i, _):
            at = pl.multiple_of(side * 1024 + i * 256, 256)
            hit = (iota((256, Q), 0) + at == answer_slot).astype(F32)
            w = st[pl.ds(at, 256), :] * factor - hit
            st[pl.ds(at, 256), :] = w
            w = w.astype(BF16)
            wt[0, pl.ds(at, 256), :] = w
            wt[1, pl.ds(at, 256), :] = mm(swap, w).astype(BF16)
            return 0

        lax.fori_loop(0, NX, one, 0)

    def grads(j, side):
        def one(i, _):
            at = pl.multiple_of(side * 1024 + i * 256, 256)
            part = mm(wt[j // 2, pl.ds(at, 256), :], q_ref[:, j * 256:(j + 1) * 256])
            gpb[j, side, i] = part.reshape(8, 32, 256)
            return 0

        lax.fori_loop(0, NX, one, 0)

    order = (1, 3, 0, 2)
    weigh(1 - core)
    for j in order:
        grads(j, 1 - core)
        rcopy(gpb.at[j, 1 - core], rc.at[j], s_rc.at[j], r_rc.at[j], sibling).start()
    weigh(core)
    grads(order[0], core)

    def along(axis, i):
        return (
            device((x + i + NX) % NX, y, z, core) if axis == "x"
            else device(x, (y + i + NY) % NY, z, core) if axis == "y"
            else device(x, y, (z + i + NZ) % NZ, core)
        )

    where = {"x": x, "y": y, "z": z}

    def ring(j):
        axis = "xyxz"[j]
        n = NX if axis == "x" else 8
        o = j // 2

        def own(half, target):
            t = (where[axis] + target + n) % n
            if axis == "x":
                return gpb.at[j, core, t, pl.ds(half * 4, 4)]
            return gpb.at[j, core, pl.ds(half * 2, 2), t]

        def held(half, way, hop):
            return (r1x if axis == "x" else r1a).at[o, half, way, hop]

        def hops(half, way):
            return n // 2 if half == way else n // 2 - 1

        return axis, own, held, hops

    def send(j, hop):
        axis, own, held, hops = ring(j)
        for half in range(2):
            for way in range(2):
                length, sign = hops(half, way), 1 - 2 * way
                if hop >= length:
                    continue
                if hop == 0:
                    source = own(half, sign * length)
                else:
                    source = held(half, way, hop - 1)
                    rcopy(
                        source, source, s_1.at[j, half, way, hop - 1], r_1.at[j, half, way, hop - 1], sibling
                    ).wait_recv()
                    source[...] = source[...] + own(half, sign * (length - hop))[...]
                rcopy(
                    source, held(half, way, hop), s_1.at[j, half, way, hop], r_1.at[j, half, way, hop],
                    along(axis, sign),
                ).start()

    def arrived(j, half):
        axis, own, held, hops = ring(j)
        acc = own(half, 0)[...]
        for way in range(2):
            hop = hops(half, way) - 1
            ref = held(half, way, hop)
            rcopy(ref, ref, s_1.at[j, half, way, hop], r_1.at[j, half, way, hop], sibling).wait_recv()
            acc = acc + ref[...]
        return acc

    for place, j in enumerate(order):
        if place:
            grads(j, core)
        rcopy(gpb.at[j, 1 - core], rc.at[j], s_rc.at[j], r_rc.at[j], sibling).wait_recv()

        def add(i, _, j=j):
            gpb[j, core, i] = gpb[j, core, i] + rc[j, i]
            return 0

        lax.fori_loop(0, NX, add, 0)
        send(j, 0)

    def queries_half(half_at):
        cols = slice(half_at * 512, (half_at + 1) * 512)

        def passages(t, acc):
            at = pl.multiple_of(t * 256, 256)
            w = jnp.transpose(st[pl.ds(at, 256), :]).astype(BF16)
            return acc + mm(w, pall[pl.ds(at, 256), cols])

        def negatives(t, acc):
            at = pl.multiple_of(t * 256, 256)
            w = jnp.transpose(jnp.exp(hs[pl.ds(at, 256), :] - lse)).astype(BF16)
            return acc + mm(w, fn[pl.ds(at, 256), cols])

        acc = lax.fori_loop(0, NP // 256, passages, jnp.zeros((Q, 512), F32))
        acc = lax.fori_loop(0, SLOTS // 256, negatives, acc)
        gq_ref[:, cols] = acc

    queries_half(0)
    for j in order:
        send(j, 1)
    queries_half(1)
    for j in (1, 3):
        send(j, 2)
    for j in (0, 2):
        o = j // 2
        a = "yz"[o]
        for half in range(2):
            ax[o, pl.ds(half * 4, 4)] = arrived(j, half)
        for i in range(1, 8):
            rcopy(
                ax.at[o, (where[a] + i) % 8], r2a.at[o, i - 1], s_2.at[j], r_2.at[j], along(a, i)
            ).start()
    for j in (1, 3):
        send(j, 3)
    for j in (1, 3):
        o = j // 2
        for half in range(2):
            aa[o, pl.ds(half * 2, 2)] = arrived(j, half)
        for i in range(1, NX):
            rcopy(
                aa.at[o, (x + i) % NX], r2x.at[o, i - 1], s_2.at[j], r_2.at[j], along("x", i)
            ).start()

    for j in (0, 2, 1, 3):
        o, first_x = j // 2, j % 2 == 0
        a, b = "yz"[o], "zy"[o]
        if first_x:
            rcopy(r2a.at[o], r2a.at[o], s_2.at[j], r_2.at[j], sibling).wait_recv()
            acc = ax[o, where[a]]
            for i in range(7):
                acc = acc + r2a[o, i]
        else:
            rcopy(r2x.at[o], r2x.at[o], s_2.at[j], r_2.at[j], sibling).wait_recv()
            acc = aa[o, x]
            for i in range(NX - 1):
                acc = acc + r2x[o, i]
        for i in range(8):
            a3[j, i] = acc[i * 4:(i + 1) * 4, :]
        for i in range(1, 8):
            rcopy(
                a3.at[j, (where[b] + i) % 8], r3.at[j, i - 1], s_3.at[j], r_3.at[j], along(b, i)
            ).start()

    for j in range(4):
        b = "zy"[j // 2]
        rcopy(r3.at[j], r3.at[j], s_3.at[j], r_3.at[j], sibling).wait_recv()
        acc = a3[j, where[b]]
        for i in range(7):
            acc = acc + r3[j, i]
        gp_ref[:, j * 256:(j + 1) * 256] = acc

    def left(ref, sem):
        rcopy(ref, ref, sem, sem, sibling).wait_send()

    left(asked.at[pl.ds(0, NZ - 1)], s_req)
    left(reqin.at[pl.ds(0, 15)], s_pass)
    gone(CHUNKS - 2)
    gone(CHUNKS - 1)
    left(zbuf.at[pl.ds(0, NZ - 1)], s_ag.at[0])
    for n in range(2):
        for hop in range(4):
            left(pall.at[pl.ds(0, 16 if hop == 3 else 32)], s_y.at[n, hop])
    for n in range(2):
        left(pall.at[pl.ds(0, 256)], s_ag.at[2 + n])
        left(pall.at[pl.ds(0, 128)], s_ag.at[4 + n])
    left(pall.at[pl.ds(0, 1024)], s_ag.at[6])
    for j in range(4):
        o, first_x = j // 2, j % 2 == 0
        left(rc.at[j], s_rc.at[j])
        _, _, held, hops = ring(j)
        for half in range(2):
            for way in range(2):
                for hop in range(hops(half, way)):
                    left(held(half, way, hop), s_1.at[j, half, way, hop])
        left(r2a.at[o] if first_x else r2x.at[o], s_2.at[j])
        left(r3.at[j], s_3.at[j])


def shards(queries, passages, negatives, neg_ids, positives):
    vmem = pl.BlockSpec(memory_space=pltpu.VMEM)
    dma = pltpu.SemaphoreType.DMA
    req, slots = pl.pallas_call(
        requests,
        out_shape=(
            jax.ShapeDtypeStruct((NZ, 16, 1, 128), I32),
            jax.ShapeDtypeStruct((8, Q), I32),
        ),
        in_specs=[vmem],
        out_specs=(vmem, vmem),
    )(neg_ids.T)
    sums = pl.pallas_call(
        kernel,
        out_shape=(
            jax.ShapeDtypeStruct((Q, D), F32),
            jax.ShapeDtypeStruct((4, D), F32),
        ),
        in_specs=[vmem] * 6,
        out_specs=(vmem, vmem),
        scratch_shapes=[
            pltpu.VMEM((NZ, 16, 1, 128), I32),
            pltpu.VMEM((16, 1, 128), I32),
            pltpu.VMEM((16, 1, 128), I32),
            pltpu.SMEM((16, 1, 128), I32),
            pltpu.VMEM((ROWS, C8, 128), F32),
            pltpu.VMEM((NB * SLAB, 128), BF16),
            pltpu.VMEM((NB * SLAB, 128), BF16),
            pltpu.VMEM((PER * SLAB, 128), F32),
            pltpu.VMEM((SLOTS, D), BF16),
            pltpu.VMEM((NP, Q), F32),
            pltpu.VMEM((SLOTS, Q), F32),
            pltpu.VMEM((32, 128), F32),
            pltpu.VMEM((32, 128), BF16),
            pltpu.VMEM((NZ, 32, 128), BF16),
            pltpu.VMEM((NZ * 32, 128), F32),
            pltpu.VMEM((NP, D), BF16),
            pltpu.VMEM((2, NP, Q), BF16),
            pltpu.VMEM((4, 2, NX, 8, 32, 256), F32),
            pltpu.VMEM((4, NX, 8, 32, 256), F32),
            pltpu.VMEM((2, 2, 2, 2, 4, 32, 256), F32),
            pltpu.VMEM((2, 2, 2, 4, 2, 32, 256), F32),
            pltpu.VMEM((2, 8, 32, 256), F32),
            pltpu.VMEM((2, NX, 32, 256), F32),
            pltpu.VMEM((2, NX - 1, 32, 256), F32),
            pltpu.VMEM((2, 7, 32, 256), F32),
            pltpu.VMEM((4, 8, 4, 256), F32),
            pltpu.VMEM((4, 7, 4, 256), F32),
            dma, dma, dma((2, 4)), dma((CHUNKS,)), dma((7,)), dma, dma, dma((2, 4)), dma((GROUPS,)), dma((7,)),
            dma((4,)), dma((4,)), dma((4, 2, 2, 4)), dma((4, 2, 2, 4)),
            dma((4,)), dma((4,)), dma((4,)), dma((4,)), dma,
        ],
        compiler_params=pltpu.CompilerParams(
            collective_id=0, has_side_effects=True, vmem_limit_bytes=58 * 1024 * 1024
        ),
        cost_estimate=pl.CostEstimate(flops=4 * Q * NP * D * 2, bytes_accessed=1 << 24, transcendentals=0),
    )(req, slots, positives.reshape(1, Q), passages, queries, negatives)
    return pl.pallas_call(
        scaled,
        out_shape=(
            jax.ShapeDtypeStruct((Q, D), F32),
            jax.ShapeDtypeStruct((4, D), F32),
        ),
        in_specs=[vmem] * 2,
        out_specs=(vmem, vmem),
    )(*sums)


def solution(mesh):
    rows = P(("blk", "grp"), None)
    return jax.shard_map(
        shards,
        mesh=mesh,
        in_specs=(rows, rows, rows, rows, P(("blk", "grp"))),
        out_specs=(rows, rows),
        check_vma=False,
    )
```

```python
import functools
import math

import jax
import jax.numpy as jnp
from jax import lax
from jax.experimental import pallas as pl
from jax.experimental.pallas import tpu as pltpu
from jax.sharding import PartitionSpec as P

MESH = pl.DeviceIdType.MESH
F32, BF16, I32 = jnp.float32, jnp.bfloat16, jnp.int32

NX, NY, NZ, NYL = 4, 8, 8, 4
NB = 128
MUL, INV = 37, 45
CAP = 10
Q, D, HARD, ROWS = 128, 1024, 7, 896
C8 = D // 128
SLAB = CAP * C8
GROUPS = 8
PER = NB // GROUPS
CHUNKS = 16
STEPS = NB // CHUNKS
VIA = 12
SLOTS = NB * CAP
NP = 2048
SCALE = 3.0 / math.sqrt(D)
NEG = -1e30


def device(x, y, z, core):
    return (((y % NYL) * NX + x) * NZ + z, (y // NYL) * 2 + core)


def rcopy(src, dst, send, recv, dev):
    return pltpu.make_async_remote_copy(
        src_ref=src, dst_ref=dst, send_sem=send, recv_sem=recv, device_id=dev, device_id_type=MESH
    )


def nt(left, right):
    return lax.dot_general(left, right, (((1,), (1,)), ((), ())), preferred_element_type=F32)


def mm(left, right):
    return lax.dot_general(left, right, (((1,), (0,)), ((), ())), preferred_element_type=F32)


def iota(shape, dim):
    return lax.broadcasted_iota(I32, shape, dim)


def requests(ids_ref, req, slots):
    mb = lax.axis_index("blk")
    sub = iota((128, Q), 0)
    before = (iota((Q, Q), 0) < iota((Q, Q), 1)).astype(F32).astype(BF16)
    base = jnp.zeros((NB, 1), F32)
    want_hi = jnp.zeros((NB, 128), F32)
    want_lo = jnp.zeros((NB, 128), F32)
    slots[...] = jnp.full((8, Q), -1, I32)
    for k in range(HARD):
        ids = ids_ref[k:k + 1, :]
        dev = jnp.floor((ids.astype(F32) + 0.5) * (1.0 / ROWS)).astype(I32)
        row = ids - dev * ROWS
        off = (dev >> 2) ^ mb
        kz, kxy = off & (NZ - 1), off >> 3
        step = (off * INV) & (NB - 1)
        hot = (sub == kz * 16 + kxy).astype(F32)
        hot16 = hot.astype(BF16)
        rank = jnp.sum(hot * (mm(hot16, before) + base), axis=0, keepdims=True).astype(I32)
        base = base + jnp.sum(hot, axis=1, keepdims=True)
        slots[k:k + 1, :] = step * CAP + rank
        at_lane = (sub == kz * 16 + rank).astype(F32)
        want_hi = want_hi + nt(hot16, (at_lane * (row >> 3).astype(F32)).astype(BF16))
        want_lo = want_lo + nt(hot16, (at_lane * (row & 7).astype(F32)).astype(BF16))
    req[...] = (want_hi * 8.0 + want_lo).astype(I32).reshape(NZ, 16, 1, 128)


def scaled(gq_in, gp_in, gq_ref, gp_ref):
    gq_ref[...] = gq_in[...] * SCALE
    gp_ref[...] = gp_in[...] * SCALE


def kernel(
    req, slots, pos_ref, pas_ref, q_ref, neg_ref,
    gq_ref, gp_ref,
    asked, passed, reqin, idsm, tab, g, f, fs, fn, st, hs, pst, pmine, zbuf, zf, pall,
    gv, hv, wt, gpb, rc, r1x, r1a, ax, aa, r2x, r2a, a3, r3,
    s_req, s_pass, s_y, s_row, s_ag, r_req, r_pass, r_y, r_row, r_ag, s_rc, r_rc, s_1, r_1, s_2, r_2, s_3, r_3, s_loc, s_via, r_via,
):
    mb = lax.axis_index("blk")
    mg = lax.axis_index("grp")
    yl, x, z = mb // (NX * NZ), (mb // NZ) % NX, mb % NZ
    yh, core = mg // 2, mg % 2
    y = yh * NYL + yl

    def partner(step):
        return (mb ^ ((step * MUL) & (NB - 1)), mg)

    sibling = device(x, y, z, 1 - core)

    barrier = pltpu.get_barrier_semaphore()

    def greet(dev):
        pl.semaphore_signal(barrier, inc=1, device_id=dev, device_id_type=MESH)

    for i in range(1, NZ):
        greet((mb ^ i, mg))
    for n in range(1, 16):
        greet((mb ^ (n * NZ), mg))
    for i in range(NYL):
        greet(device(x, (1 - yh) * NYL + i, z, core))
    greet(sibling)

    for c in range(C8):
        pst[pl.ds(c, 4, stride=C8), :] = pas_ref[:, c * 128:(c + 1) * 128].astype(F32)
    own = pst[...].astype(BF16)
    pmine[...] = own
    zbuf[z] = own

    pl.semaphore_wait(barrier, NZ - 1 + 15 + NYL + 1)

    for i in range(1, NZ):
        rcopy(req.at[i], asked.at[i], s_req, r_req, (mb ^ i, mg)).start()
    asked[0] = req[0]

    for i in range(1, NZ):
        to = device(x, y, (z + i) % NZ, core)
        rcopy(pmine, zbuf.at[z], s_ag.at[0], r_ag.at[0], to).start()

    rcopy(asked.at[pl.ds(0, NZ - 1)], asked.at[pl.ds(0, NZ - 1)], s_req, r_req, sibling).wait_recv()
    total = asked[0]
    for i in range(1, NZ):
        total = total + asked[i]
    passed[...] = total
    for n in range(1, 16):
        rcopy(passed.at[n], reqin.at[n], s_pass, r_pass, (mb ^ (n * NZ), mg)).start()
    reqin[0] = passed[0]

    flat = tab.reshape(ROWS * C8, 128)
    for t in range(ROWS // 128):
        for c in range(C8):
            part = neg_ref[t * 128:(t + 1) * 128, c * 128:(c + 1) * 128].astype(F32)
            flat[pl.ds(t * 1024 + c, 128, stride=C8), :] = part

    rcopy(zbuf.at[pl.ds(0, NZ - 1)], zbuf.at[pl.ds(0, NZ - 1)], s_ag.at[0], r_ag.at[0], sibling).wait_recv()
    zf[...] = zbuf[...].reshape(NZ * 32, 128).astype(F32)
    mine = pl.multiple_of(((core * NX + x) * NY + y) * 32, 32)
    for c in range(C8):
        pall[pl.ds(mine, 32), c * 128:(c + 1) * 128] = zf[pl.ds(c, 32, stride=C8), :].astype(BF16)

    def along_y(hop):
        for n in range(2):
            sign = 1 - 2 * n
            rows = 16 if hop == 3 else 32
            at = ((core * NX + x) * NY + (y + NY - sign * hop) % NY) * 32 + (16 * n if hop == 3 else 0)
            block = pall.at[pl.ds(pl.multiple_of(at, 16), rows)]
            if hop:
                came = pall.at[pl.ds(0, 32)]
                rcopy(came, came, s_y.at[n, hop - 1], r_y.at[n, hop - 1], sibling).wait_recv()
            to = device(x, (y + NY + sign) % NY, z, core)
            rcopy(block, block, s_y.at[n, hop], r_y.at[n, hop], to).start()

    along_y(0)

    rcopy(reqin.at[pl.ds(0, 15)], reqin.at[pl.ds(0, 15)], s_pass, r_pass, sibling).wait_recv()
    local = pltpu.make_async_copy(reqin, idsm, s_loc)
    local.start()
    local.wait()

    def pick(step, dst, at):
        k = (step * MUL) % NB
        n, lane = k // NZ, (k % NZ) * 16
        for j in range(CAP // 2):
            pair = jnp.concatenate([tab[idsm[n, 0, lane + 2 * j]], tab[idsm[n, 0, lane + 2 * j + 1]]], axis=0)
            dst[pl.ds(at + 16 * j, 16), :] = pair.astype(BF16)

    def answer(step, _):
        at = pl.multiple_of(step * SLAB, 16)
        pick(step, g, at)
        rcopy(
            g.at[pl.ds(at, SLAB)], f.at[pl.ds(at, SLAB)], s_row.at[step // STEPS], r_row.at[step // PER], partner(step)
        ).start()
        return 0

    def gather_via(u, _):
        pick(u * PER + VIA, gv, pl.multiple_of(u * SLAB, 16))
        return 0

    def pass_on(u, _):
        step = u * PER + VIA
        source = mb - z + (z + 1) % NZ
        to = (source ^ ((step * MUL) & (NB - 1)), mg)
        block = hv.at[pl.ds(pl.multiple_of(u * SLAB, 16), SLAB)]
        at = pl.multiple_of(step * SLAB, 16)
        rcopy(block, f.at[pl.ds(at, SLAB)], s_via.at[1], r_row.at[u], to).start()
        return 0

    def gone(chunk):
        ref = f.at[pl.ds(0, (STEPS - (1 if chunk == 0 or chunk % 2 else 0)) * SLAB)]
        rcopy(ref, ref, s_row.at[chunk], s_row.at[chunk], sibling).wait_send()

    def answers(chunk):
        first, last = max(1, chunk * STEPS), (chunk + 1) * STEPS
        if chunk % 2:
            lax.fori_loop(first, chunk // 2 * PER + VIA, answer, 0)
            first = chunk // 2 * PER + VIA + 1
        lax.fori_loop(first, last, answer, 0)
        if chunk >= 2:
            gone(chunk - 2)

    right, left_x = device((x + 1) % NX, y, z, core), device((x + NX - 1) % NX, y, z, core)

    def slab(at, rows, extra=0):
        return pall.at[pl.ds(pl.multiple_of((core * NX + at) * 256 + extra, 128), rows)]

    def along_x(hop):
        for n, to in ((0, right), (1, left_x)):
            if hop == 0:
                came = pall.at[pl.ds(0, 16)]
                rcopy(came, came, s_y.at[n, 3], r_y.at[n, 3], sibling).wait_recv()
        for n, to in ((0, right), (1, left_x)):
            if hop == 0:
                rcopy(slab(x, 256), slab(x, 256), s_ag.at[2 + n], r_ag.at[2 + n], to).start()
            else:
                came = (x + NX - 1) % NX if n == 0 else (x + 1) % NX
                rcopy(slab(came, 256), slab(came, 256), s_ag.at[2 + n], r_ag.at[2 + n], to).wait_recv()
                part = slab(came, 128, 128 * n)
                rcopy(part, part, s_ag.at[4 + n], r_ag.at[4 + n], to).start()

    half = pall.at[pl.ds(pl.multiple_of(core * 1024, 1024), 1024)]

    def across():
        for n in range(2):
            part = slab((x + 2) % NX, 128, 128 * n)
            rcopy(part, part, s_ag.at[4 + n], r_ag.at[4 + n], sibling).wait_recv()
        rcopy(half, half, s_ag.at[6], r_ag.at[6], sibling).start()

    def score(t, top):
        at = pl.multiple_of(t * 256, 256)
        part = nt(pall[pl.ds(at, 256), :], q_ref[...]) * SCALE
        st[pl.ds(at, 256), :] = part
        return jnp.maximum(top, jnp.max(part, axis=0, keepdims=True))

    def raise_(t, carry):
        pool_top, total = carry
        at = pl.multiple_of(t * 256, 256)
        part = jnp.exp(st[pl.ds(at, 256), :] - pool_top)
        st[pl.ds(at, 256), :] = part
        return pool_top, total + jnp.sum(part, axis=0, keepdims=True)

    def pool():
        rcopy(half, half, s_ag.at[6], r_ag.at[6], sibling).wait_recv()
        pool_top = lax.fori_loop(0, NP // 256, score, jnp.full((1, Q), NEG, F32))
        return lax.fori_loop(0, NP // 256, raise_, (pool_top, jnp.zeros((1, Q), F32)))

    def hard(group, top):
        at = pl.multiple_of(group * PER * SLAB, PER * SLAB)
        row0 = pl.multiple_of(group * PER * CAP, PER * CAP)
        fs[...] = f[pl.ds(at, PER * SLAB), :].astype(F32)
        for c in range(C8):
            fn[pl.ds(row0, PER * CAP), c * 128:(c + 1) * 128] = fs[
                pl.ds(c, PER * CAP, stride=C8), :
            ].astype(BF16)
        part = nt(fn[pl.ds(row0, PER * CAP), :], q_ref[...]) * SCALE
        number = iota((PER * CAP, Q), 0) + row0
        taken = number == slots[0:1, :]
        for k in range(1, HARD):
            taken = taken | (number == slots[k:k + 1, :])
        part = jnp.where(taken, part, NEG)
        hs[pl.ds(row0, PER * CAP), :] = part
        return jnp.maximum(top, jnp.max(part, axis=0, keepdims=True))

    def group_in(group, top):
        n = PER - (1 if group == 0 else 0)
        ref = f.at[pl.ds(0, n * SLAB)]
        rcopy(ref, ref, s_pass, r_row.at[group], sibling).wait_recv()
        return hard(group, top)

    hard_top = jnp.full((1, Q), NEG, F32)
    lax.fori_loop(0, GROUPS, gather_via, 0)
    rcopy(gv, hv, s_via.at[0], r_via, device(x, y, (z + NZ - 1) % NZ, core)).start()
    along_y(1)
    for chunk in range(CHUNKS):
        answers(chunk)
        if chunk == 0:
            pick(0, f, 0)
            along_y(2)
        elif chunk == 1:
            along_y(3)
        elif chunk == 2:
            rcopy(gv, hv, s_via.at[0], r_via, sibling).wait_recv()
            lax.fori_loop(0, GROUPS, pass_on, 0)
            along_x(0)
        elif chunk == 5:
            along_x(1)
        elif chunk == 7:
            across()
        elif chunk == 10:
            pool_top, pool_total = pool()
        if chunk >= 5 and chunk % 2 == 1:
            hard_top = group_in((chunk - 5) // 2, hard_top)
    for group in range((CHUNKS - 4) // 2, GROUPS):
        hard_top = group_in(group, hard_top)
    top = jnp.maximum(pool_top, hard_top)

    total = pool_total * jnp.exp(pool_top - top) + jnp.sum(jnp.exp(hs[...] - top), axis=0, keepdims=True)
    lse = top + jnp.log(total)
    factor = jnp.exp(pool_top - lse)

    p = pos_ref[...]
    answer_slot = (
        (((p >> 2) & 1) << 10)
        | (((p >> 7) & 3) << 8)
        | (((p >> 3) & 1) << 7)
        | (((p >> 9) & 3) << 5)
        | (((p >> 4) & 7) << 2)
        | (p & 3)
    )
    there = iota((256, 256), 0)
    source = (((there >> 2) & 7) << 5) | ((there >> 5) << 2) | (there & 3)
    swap = (iota((256, 256), 1) == source).astype(F32).astype(BF16)

    def weigh(side):
        def one(i, _):
            at = pl.multiple_of(side * 1024 + i * 256, 256)
            hit = (iota((256, Q), 0) + at == answer_slot).astype(F32)
            w = st[pl.ds(at, 256), :] * factor - hit
            st[pl.ds(at, 256), :] = w
            w = w.astype(BF16)
            wt[0, pl.ds(at, 256), :] = w
            wt[1, pl.ds(at, 256), :] = mm(swap, w).astype(BF16)
            return 0

        lax.fori_loop(0, NX, one, 0)

    def grads(j, side):
        def one(i, _):
            at = pl.multiple_of(side * 1024 + i * 256, 256)
            part = mm(wt[j // 2, pl.ds(at, 256), :], q_ref[:, j * 256:(j + 1) * 256])
            gpb[j, side, i] = part.reshape(8, 32, 256)
            return 0

        lax.fori_loop(0, NX, one, 0)

    order = (0, 1, 3, 2)
    weigh(1 - core)
    for j in order:
        grads(j, 1 - core)
        rcopy(gpb.at[j, 1 - core], rc.at[j], s_rc.at[j], r_rc.at[j], sibling).start()
    weigh(core)
    grads(order[0], core)

    def along(axis, i):
        return (
            device((x + i + NX) % NX, y, z, core) if axis == "x"
            else device(x, (y + i + NY) % NY, z, core) if axis == "y"
            else device(x, y, (z + i + NZ) % NZ, core)
        )

    where = {"x": x, "y": y, "z": z}

    def ring(j):
        axis = "xyxz"[j]
        n = NX if axis == "x" else 8
        o = j // 2

        def own(half, target):
            t = (where[axis] + target + n) % n
            if axis == "x":
                return gpb.at[j, core, t, pl.ds(half * 4, 4)]
            return gpb.at[j, core, pl.ds(half * 2, 2), t]

        def held(half, way, hop):
            return (r1x if axis == "x" else r1a).at[o, half, way, hop]

        def hops(half, way):
            return n // 2 if half == way else n // 2 - 1

        return axis, own, held, hops

    def send(j, hop):
        axis, own, held, hops = ring(j)
        for half, way in ((0, 0), (1, 1), (1, 0), (0, 1)):
            length, sign = hops(half, way), 1 - 2 * way
            if hop >= length:
                continue
            if hop == 0:
                source = own(half, sign * length)
            else:
                source = held(half, way, hop - 1)
                rcopy(
                    source, source, s_1.at[j, half, way, hop - 1], r_1.at[j, half, way, hop - 1], sibling
                ).wait_recv()
                source[...] = source[...] + own(half, sign * (length - hop))[...]
            rcopy(
                source, held(half, way, hop), s_1.at[j, half, way, hop], r_1.at[j, half, way, hop],
                along(axis, sign),
            ).start()

    def arrived(j, half):
        axis, own, held, hops = ring(j)
        acc = own(half, 0)[...]
        for way in range(2):
            hop = hops(half, way) - 1
            ref = held(half, way, hop)
            rcopy(ref, ref, s_1.at[j, half, way, hop], r_1.at[j, half, way, hop], sibling).wait_recv()
            acc = acc + ref[...]
        return acc

    for place, j in enumerate(order):
        if place:
            grads(j, core)
        rcopy(gpb.at[j, 1 - core], rc.at[j], s_rc.at[j], r_rc.at[j], sibling).wait_recv()

        def add(i, _, j=j):
            gpb[j, core, i] = gpb[j, core, i] + rc[j, i]
            return 0

        lax.fori_loop(0, NX, add, 0)
        send(j, 0)

    def queries_half(half_at):
        cols = slice(half_at * 512, (half_at + 1) * 512)

        def passages(t, acc):
            at = pl.multiple_of(t * 256, 256)
            w = jnp.transpose(st[pl.ds(at, 256), :]).astype(BF16)
            return acc + mm(w, pall[pl.ds(at, 256), cols])

        def negatives(t, acc):
            at = pl.multiple_of(t * 256, 256)
            w = jnp.transpose(jnp.exp(hs[pl.ds(at, 256), :] - lse)).astype(BF16)
            return acc + mm(w, fn[pl.ds(at, 256), cols])

        acc = lax.fori_loop(0, NP // 256, passages, jnp.zeros((Q, 512), F32))
        acc = lax.fori_loop(0, SLOTS // 256, negatives, acc)
        gq_ref[:, cols] = acc

    queries_half(0)
    for j in order:
        send(j, 1)
    queries_half(1)
    def second(j):
        axis, o = "xyxz"[j], j // 2
        if axis == "x":
            a = "yz"[o]
            for half in range(2):
                ax[o, pl.ds(half * 4, 4)] = arrived(j, half)
            for i in range(1, 8):
                rcopy(
                    ax.at[o, (where[a] + i) % 8], r2a.at[o, i - 1], s_2.at[j], r_2.at[j], along(a, i)
                ).start()
        else:
            for half in range(2):
                aa[o, pl.ds(half * 2, 2)] = arrived(j, half)
            for i in range(1, NX):
                rcopy(
                    aa.at[o, (x + i) % NX], r2x.at[o, i - 1], s_2.at[j], r_2.at[j], along("x", i)
                ).start()

    send(1, 2)
    send(3, 2)
    second(0)
    send(1, 3)
    send(3, 3)
    second(2)
    second(1)
    second(3)

    for j in (0, 2, 1, 3):
        o, first_x = j // 2, j % 2 == 0
        a, b = "yz"[o], "zy"[o]
        if first_x:
            rcopy(r2a.at[o], r2a.at[o], s_2.at[j], r_2.at[j], sibling).wait_recv()
            acc = ax[o, where[a]]
            for i in range(7):
                acc = acc + r2a[o, i]
        else:
            rcopy(r2x.at[o], r2x.at[o], s_2.at[j], r_2.at[j], sibling).wait_recv()
            acc = aa[o, x]
            for i in range(NX - 1):
                acc = acc + r2x[o, i]
        for i in range(8):
            a3[j, i] = acc[i * 4:(i + 1) * 4, :]
        for i in range(1, 8):
            rcopy(
                a3.at[j, (where[b] + i) % 8], r3.at[j, i - 1], s_3.at[j], r_3.at[j], along(b, i)
            ).start()

    for j in range(4):
        b = "zy"[j // 2]
        rcopy(r3.at[j], r3.at[j], s_3.at[j], r_3.at[j], sibling).wait_recv()
        acc = a3[j, where[b]]
        for i in range(7):
            acc = acc + r3[j, i]
        gp_ref[:, j * 256:(j + 1) * 256] = acc

    def left(ref, sem):
        rcopy(ref, ref, sem, sem, sibling).wait_send()

    left(asked.at[pl.ds(0, NZ - 1)], s_req)
    left(reqin.at[pl.ds(0, 15)], s_pass)
    left(hv, s_via.at[0])
    left(hv, s_via.at[1])
    gone(CHUNKS - 2)
    gone(CHUNKS - 1)
    left(zbuf.at[pl.ds(0, NZ - 1)], s_ag.at[0])
    for n in range(2):
        for hop in range(4):
            left(pall.at[pl.ds(0, 16 if hop == 3 else 32)], s_y.at[n, hop])
    for n in range(2):
        left(pall.at[pl.ds(0, 256)], s_ag.at[2 + n])
        left(pall.at[pl.ds(0, 128)], s_ag.at[4 + n])
    left(pall.at[pl.ds(0, 1024)], s_ag.at[6])
    for j in range(4):
        o, first_x = j // 2, j % 2 == 0
        left(rc.at[j], s_rc.at[j])
        _, _, held, hops = ring(j)
        for half in range(2):
            for way in range(2):
                for hop in range(hops(half, way)):
                    left(held(half, way, hop), s_1.at[j, half, way, hop])
        left(r2a.at[o] if first_x else r2x.at[o], s_2.at[j])
        left(r3.at[j], s_3.at[j])


def shards(queries, passages, negatives, neg_ids, positives):
    vmem = pl.BlockSpec(memory_space=pltpu.VMEM)
    dma = pltpu.SemaphoreType.DMA
    req, slots = pl.pallas_call(
        requests,
        out_shape=(
            jax.ShapeDtypeStruct((NZ, 16, 1, 128), I32),
            jax.ShapeDtypeStruct((8, Q), I32),
        ),
        in_specs=[vmem],
        out_specs=(vmem, vmem),
    )(neg_ids.T)
    sums = pl.pallas_call(
        kernel,
        out_shape=(
            jax.ShapeDtypeStruct((Q, D), F32),
            jax.ShapeDtypeStruct((4, D), F32),
        ),
        in_specs=[vmem] * 6,
        out_specs=(vmem, vmem),
        scratch_shapes=[
            pltpu.VMEM((NZ, 16, 1, 128), I32),
            pltpu.VMEM((16, 1, 128), I32),
            pltpu.VMEM((16, 1, 128), I32),
            pltpu.SMEM((16, 1, 128), I32),
            pltpu.VMEM((ROWS, C8, 128), F32),
            pltpu.VMEM((NB * SLAB, 128), BF16),
            pltpu.VMEM((NB * SLAB, 128), BF16),
            pltpu.VMEM((PER * SLAB, 128), F32),
            pltpu.VMEM((SLOTS, D), BF16),
            pltpu.VMEM((NP, Q), F32),
            pltpu.VMEM((SLOTS, Q), F32),
            pltpu.VMEM((32, 128), F32),
            pltpu.VMEM((32, 128), BF16),
            pltpu.VMEM((NZ, 32, 128), BF16),
            pltpu.VMEM((NZ * 32, 128), F32),
            pltpu.VMEM((NP, D), BF16),
            pltpu.VMEM((GROUPS * SLAB, 128), BF16),
            pltpu.VMEM((GROUPS * SLAB, 128), BF16),
            pltpu.VMEM((2, NP, Q), BF16),
            pltpu.VMEM((4, 2, NX, 8, 32, 256), F32),
            pltpu.VMEM((4, NX, 8, 32, 256), F32),
            pltpu.VMEM((2, 2, 2, 2, 4, 32, 256), F32),
            pltpu.VMEM((2, 2, 2, 4, 2, 32, 256), F32),
            pltpu.VMEM((2, 8, 32, 256), F32),
            pltpu.VMEM((2, NX, 32, 256), F32),
            pltpu.VMEM((2, NX - 1, 32, 256), F32),
            pltpu.VMEM((2, 7, 32, 256), F32),
            pltpu.VMEM((4, 8, 4, 256), F32),
            pltpu.VMEM((4, 7, 4, 256), F32),
            dma, dma, dma((2, 4)), dma((CHUNKS,)), dma((7,)), dma, dma, dma((2, 4)), dma((GROUPS,)), dma((7,)),
            dma((4,)), dma((4,)), dma((4, 2, 2, 4)), dma((4, 2, 2, 4)),
            dma((4,)), dma((4,)), dma((4,)), dma((4,)), dma, dma((2,)), dma,
        ],
        compiler_params=pltpu.CompilerParams(
            collective_id=0, has_side_effects=True, vmem_limit_bytes=58 * 1024 * 1024
        ),
        cost_estimate=pl.CostEstimate(flops=4 * Q * NP * D * 2, bytes_accessed=1 << 24, transcendentals=0),
    )(req, slots, positives.reshape(1, Q), passages, queries, negatives)
    return pl.pallas_call(
        scaled,
        out_shape=(
            jax.ShapeDtypeStruct((Q, D), F32),
            jax.ShapeDtypeStruct((4, D), F32),
        ),
        in_specs=[vmem] * 2,
        out_specs=(vmem, vmem),
    )(*sums)


def solution(mesh):
    rows = P(("blk", "grp"), None)
    return jax.shard_map(
        shards,
        mesh=mesh,
        in_specs=(rows, rows, rows, rows, P(("blk", "grp"))),
        out_specs=(rows, rows),
        check_vma=False,
    )
```

```python
import functools
import math

import jax
import jax.numpy as jnp
from jax import lax
from jax.experimental import pallas as pl
from jax.experimental.pallas import tpu as pltpu
from jax.sharding import PartitionSpec as P

MESH = pl.DeviceIdType.MESH
F32, BF16, I32 = jnp.float32, jnp.bfloat16, jnp.int32

NX, NY, NZ, NYL = 4, 8, 8, 4
NB = 128
MUL, INV = 37, 45
CAP = 10
Q, D, HARD, ROWS = 128, 1024, 7, 896
C8 = D // 128
SLAB = CAP * C8
GROUPS = 8
PER = NB // GROUPS
CHUNKS = 16
STEPS = NB // CHUNKS
SLOTS = NB * CAP
NP = 2048
SCALE = 3.0 / math.sqrt(D)
NEG = -1e30


def device(x, y, z, core):
    return (((y % NYL) * NX + x) * NZ + z, (y // NYL) * 2 + core)


def rcopy(src, dst, send, recv, dev):
    return pltpu.make_async_remote_copy(
        src_ref=src, dst_ref=dst, send_sem=send, recv_sem=recv, device_id=dev, device_id_type=MESH
    )


def nt(left, right):
    return lax.dot_general(left, right, (((1,), (1,)), ((), ())), preferred_element_type=F32)


def mm(left, right):
    return lax.dot_general(left, right, (((1,), (0,)), ((), ())), preferred_element_type=F32)


def iota(shape, dim):
    return lax.broadcasted_iota(I32, shape, dim)


def requests(ids_ref, req, slots):
    mb = lax.axis_index("blk")
    sub = iota((128, Q), 0)
    before = (iota((Q, Q), 0) < iota((Q, Q), 1)).astype(F32).astype(BF16)
    base = jnp.zeros((NB, 1), F32)
    want_hi = jnp.zeros((NB, 128), F32)
    want_lo = jnp.zeros((NB, 128), F32)
    slots[...] = jnp.full((8, Q), -1, I32)
    for k in range(HARD):
        ids = ids_ref[k:k + 1, :]
        dev = jnp.floor((ids.astype(F32) + 0.5) * (1.0 / ROWS)).astype(I32)
        row = ids - dev * ROWS
        off = (dev >> 2) ^ mb
        kz, kxy = off & (NZ - 1), off >> 3
        step = (off * INV) & (NB - 1)
        hot = (sub == kz * 16 + kxy).astype(F32)
        hot16 = hot.astype(BF16)
        rank = jnp.sum(hot * (mm(hot16, before) + base), axis=0, keepdims=True).astype(I32)
        base = base + jnp.sum(hot, axis=1, keepdims=True)
        slots[k:k + 1, :] = step * CAP + rank
        at_lane = (sub == kz * 16 + rank).astype(F32)
        want_hi = want_hi + nt(hot16, (at_lane * (row >> 3).astype(F32)).astype(BF16))
        want_lo = want_lo + nt(hot16, (at_lane * (row & 7).astype(F32)).astype(BF16))
    req[...] = (want_hi * 8.0 + want_lo).astype(I32).reshape(NZ, 16, 1, 128)


def scaled(gq_in, gp_in, gq_ref, gp_ref):
    gq_ref[...] = gq_in[...] * SCALE
    gp_ref[...] = gp_in[...] * SCALE


def kernel(
    req, slots, pos_ref, pas_ref, q_ref, neg_ref,
    gq_ref, gp_ref,
    asked, passed, reqin, idsm, tab, g, f, fs, fn, st, hs, pst, pmine, zbuf, zf, pall,
    qall, wt, wk, acc2, r1, a3, r3,
    s_req, s_pass, s_y, s_row, s_ag, r_req, r_pass, r_y, r_row, r_ag, s_q, r_q, s_w, r_w, s_1, r_1, s_3, r_3, s_loc,
):
    mb = lax.axis_index("blk")
    mg = lax.axis_index("grp")
    yl, x, z = mb // (NX * NZ), (mb // NZ) % NX, mb % NZ
    yh, core = mg // 2, mg % 2
    y = yh * NYL + yl

    def partner(step):
        return (mb ^ ((step * MUL) & (NB - 1)), mg)

    sibling = device(x, y, z, 1 - core)

    barrier = pltpu.get_barrier_semaphore()

    def greet(dev):
        pl.semaphore_signal(barrier, inc=1, device_id=dev, device_id_type=MESH)

    for i in range(1, NZ):
        greet((mb ^ i, mg))
    for n in range(1, 16):
        greet((mb ^ (n * NZ), mg))
    for i in range(NYL):
        greet(device(x, (1 - yh) * NYL + i, z, core))
    greet(sibling)
    for i in range(1, NX):
        greet(device((x + i) % NX, y, z, 1 - core))

    for c in range(C8):
        pst[pl.ds(c, 4, stride=C8), :] = pas_ref[:, c * 128:(c + 1) * 128].astype(F32)
    own = pst[...].astype(BF16)
    pmine[...] = own
    zbuf[z] = own

    pl.semaphore_wait(barrier, NZ - 1 + 15 + NYL + 1 + NX - 1)

    for i in range(1, NZ):
        rcopy(req.at[i], asked.at[i], s_req, r_req, (mb ^ i, mg)).start()
    asked[0] = req[0]

    for i in range(1, NZ):
        to = device(x, y, (z + i) % NZ, core)
        rcopy(pmine, zbuf.at[z], s_ag.at[0], r_ag.at[0], to).start()

    rcopy(asked.at[pl.ds(0, NZ - 1)], asked.at[pl.ds(0, NZ - 1)], s_req, r_req, sibling).wait_recv()
    total = asked[0]
    for i in range(1, NZ):
        total = total + asked[i]
    passed[...] = total
    for n in range(1, 16):
        rcopy(passed.at[n], reqin.at[n], s_pass, r_pass, (mb ^ (n * NZ), mg)).start()
    reqin[0] = passed[0]

    flat = tab.reshape(ROWS * C8, 128)
    for t in range(ROWS // 128):
        for c in range(C8):
            part = neg_ref[t * 128:(t + 1) * 128, c * 128:(c + 1) * 128].astype(F32)
            flat[pl.ds(t * 1024 + c, 128, stride=C8), :] = part

    rcopy(zbuf.at[pl.ds(0, NZ - 1)], zbuf.at[pl.ds(0, NZ - 1)], s_ag.at[0], r_ag.at[0], sibling).wait_recv()
    zf[...] = zbuf[...].reshape(NZ * 32, 128).astype(F32)
    mine = pl.multiple_of(((core * NX + x) * NY + y) * 32, 32)
    for c in range(C8):
        pall[pl.ds(mine, 32), c * 128:(c + 1) * 128] = zf[pl.ds(c, 32, stride=C8), :].astype(BF16)

    def along_y(hop):
        for n in range(2):
            sign = 1 - 2 * n
            rows = 16 if hop == 3 else 32
            at = ((core * NX + x) * NY + (y + NY - sign * hop) % NY) * 32 + (16 * n if hop == 3 else 0)
            block = pall.at[pl.ds(pl.multiple_of(at, 16), rows)]
            if hop:
                came = pall.at[pl.ds(0, 32)]
                rcopy(came, came, s_y.at[n, hop - 1], r_y.at[n, hop - 1], sibling).wait_recv()
            to = device(x, (y + NY + sign) % NY, z, core)
            rcopy(block, block, s_y.at[n, hop], r_y.at[n, hop], to).start()

    along_y(0)

    rcopy(reqin.at[pl.ds(0, 15)], reqin.at[pl.ds(0, 15)], s_pass, r_pass, sibling).wait_recv()
    local = pltpu.make_async_copy(reqin, idsm, s_loc)
    local.start()
    local.wait()

    def pick(step, dst):
        at = pl.multiple_of(step * SLAB, 16)
        k = (step * MUL) % NB
        n, lane = k // NZ, (k % NZ) * 16
        for j in range(CAP // 2):
            pair = jnp.concatenate([tab[idsm[n, 0, lane + 2 * j]], tab[idsm[n, 0, lane + 2 * j + 1]]], axis=0)
            dst[pl.ds(at + 16 * j, 16), :] = pair.astype(BF16)

    def answer(step, _):
        pick(step, g)
        at = pl.multiple_of(step * SLAB, 16)
        rcopy(
            g.at[pl.ds(at, SLAB)], f.at[pl.ds(at, SLAB)], s_row.at[step // STEPS], r_row.at[step // PER], partner(step)
        ).start()
        return 0

    def gone(chunk):
        ref = f.at[pl.ds(0, (STEPS - (1 if chunk == 0 else 0)) * SLAB)]
        rcopy(ref, ref, s_row.at[chunk], s_row.at[chunk], sibling).wait_send()

    def answers(chunk):
        lax.fori_loop(max(1, chunk * STEPS), (chunk + 1) * STEPS, answer, 0)
        if chunk >= 2:
            gone(chunk - 2)

    right, left_x = device((x + 1) % NX, y, z, core), device((x + NX - 1) % NX, y, z, core)

    def slab(at, rows, extra=0):
        return pall.at[pl.ds(pl.multiple_of((core * NX + at) * 256 + extra, 128), rows)]

    def along_x(hop):
        for n, to in ((0, right), (1, left_x)):
            if hop == 0:
                came = pall.at[pl.ds(0, 16)]
                rcopy(came, came, s_y.at[n, 3], r_y.at[n, 3], sibling).wait_recv()
        for n, to in ((0, right), (1, left_x)):
            if hop == 0:
                rcopy(slab(x, 256), slab(x, 256), s_ag.at[2 + n], r_ag.at[2 + n], to).start()
            else:
                came = (x + NX - 1) % NX if n == 0 else (x + 1) % NX
                rcopy(slab(came, 256), slab(came, 256), s_ag.at[2 + n], r_ag.at[2 + n], to).wait_recv()
                part = slab(came, 128, 128 * n)
                rcopy(part, part, s_ag.at[4 + n], r_ag.at[4 + n], to).start()

    half = pall.at[pl.ds(pl.multiple_of(core * 1024, 1024), 1024)]

    def across():
        for n in range(2):
            part = slab((x + 2) % NX, 128, 128 * n)
            rcopy(part, part, s_ag.at[4 + n], r_ag.at[4 + n], sibling).wait_recv()
        rcopy(half, half, s_ag.at[6], r_ag.at[6], sibling).start()

    def score(t, top):
        at = pl.multiple_of(t * 256, 256)
        part = nt(pall[pl.ds(at, 256), :], q_ref[...]) * SCALE
        st[pl.ds(at, 256), :] = part
        return jnp.maximum(top, jnp.max(part, axis=0, keepdims=True))

    def raise_(t, carry):
        pool_top, total = carry
        at = pl.multiple_of(t * 256, 256)
        part = jnp.exp(st[pl.ds(at, 256), :] - pool_top)
        st[pl.ds(at, 256), :] = part
        return pool_top, total + jnp.sum(part, axis=0, keepdims=True)

    def pool():
        rcopy(half, half, s_ag.at[6], r_ag.at[6], sibling).wait_recv()
        pool_top = lax.fori_loop(0, NP // 256, score, jnp.full((1, Q), NEG, F32))
        return lax.fori_loop(0, NP // 256, raise_, (pool_top, jnp.zeros((1, Q), F32)))

    def hard(group, top):
        at = pl.multiple_of(group * PER * SLAB, PER * SLAB)
        row0 = pl.multiple_of(group * PER * CAP, PER * CAP)
        fs[...] = f[pl.ds(at, PER * SLAB), :].astype(F32)
        for c in range(C8):
            fn[pl.ds(row0, PER * CAP), c * 128:(c + 1) * 128] = fs[
                pl.ds(c, PER * CAP, stride=C8), :
            ].astype(BF16)
        part = nt(fn[pl.ds(row0, PER * CAP), :], q_ref[...]) * SCALE
        number = iota((PER * CAP, Q), 0) + row0
        taken = number == slots[0:1, :]
        for k in range(1, HARD):
            taken = taken | (number == slots[k:k + 1, :])
        part = jnp.where(taken, part, NEG)
        hs[pl.ds(row0, PER * CAP), :] = part
        return jnp.maximum(top, jnp.max(part, axis=0, keepdims=True))

    def group_in(group, top):
        n = PER - (1 if group == 0 else 0)
        ref = f.at[pl.ds(0, n * SLAB)]
        rcopy(ref, ref, s_pass, r_row.at[group], sibling).wait_recv()
        return hard(group, top)

    own_slot = core * NX + x
    own_rows = qall.at[pl.ds(pl.multiple_of(own_slot * Q, Q), Q)]
    own_rows[...] = q_ref[...]

    def queries_x():
        for i in range(1, NX):
            to = device((x + i) % NX, y, z, core)
            rcopy(own_rows, own_rows, s_q.at[0], r_q.at[0], to).start()

    side_rows = qall.at[pl.ds(pl.multiple_of(core * NX * Q, NX * Q), NX * Q)]

    def queries_across():
        ref = qall.at[pl.ds(0, (NX - 1) * Q)]
        rcopy(ref, ref, s_q.at[0], r_q.at[0], sibling).wait_recv()
        rcopy(side_rows, side_rows, s_q.at[1], r_q.at[1], sibling).start()

    hard_top = jnp.full((1, Q), NEG, F32)
    along_y(1)
    for chunk in range(CHUNKS):
        answers(chunk)
        if chunk == 0:
            pick(0, f)
            along_y(2)
        elif chunk == 1:
            along_y(3)
        elif chunk == 2:
            along_x(0)
        elif chunk == 5:
            along_x(1)
        elif chunk == 7:
            across()
            queries_x()
        elif chunk == 10:
            pool_top, pool_total = pool()
        elif chunk == 13:
            queries_across()
        if chunk >= 5 and chunk % 2 == 1:
            hard_top = group_in((chunk - 5) // 2, hard_top)
    for group in range((CHUNKS - 4) // 2, GROUPS):
        hard_top = group_in(group, hard_top)
    top = jnp.maximum(pool_top, hard_top)

    total = pool_total * jnp.exp(pool_top - top) + jnp.sum(jnp.exp(hs[...] - top), axis=0, keepdims=True)
    lse = top + jnp.log(total)
    factor = jnp.exp(pool_top - lse)

    p = pos_ref[...]
    answer_slot = (
        (((p >> 2) & 1) << 10)
        | (((p >> 7) & 3) << 8)
        | (((p >> 3) & 1) << 7)
        | (((p >> 9) & 3) << 5)
        | (((p >> 4) & 7) << 2)
        | (p & 3)
    )
    there = iota((256, 256), 0)
    source = (((there >> 2) & 7) << 5) | ((there >> 5) << 2) | (there & 3)
    swap = (iota((256, 256), 1) == source).astype(F32).astype(BF16)

    def weigh(tile):
        at = pl.multiple_of(tile * 256, 256)
        hit = (iota((256, Q), 0) + at == answer_slot).astype(F32)
        w = st[pl.ds(at, 256), :] * factor - hit
        st[pl.ds(at, 256), :] = w
        return w.astype(BF16)

    for dc, dx in ((1, 2), (0, 2), (1, 1), (1, 3), (0, 1), (0, 3), (1, 0)):
        tc, tx = (core + dc) % 2, (x + dx) % NX
        tile = tc * NX + tx
        wt[tile] = weigh(tile)
        rcopy(wt.at[tile], wk.at[own_slot], s_w, r_w, device(tx, y, z, tc)).start()
    wk[own_slot] = weigh(own_slot)

    def along(axis, i):
        return (
            device((x + i + NX) % NX, y, z, core) if axis == "x"
            else device(x, (y + i + NY) % NY, z, core) if axis == "y"
            else device(x, y, (z + i + NZ) % NZ, core)
        )

    where = {"y": y, "z": z}

    def own(o, half, target):
        return acc2.at[o, (where["yz"[o]] + target + 8) % 8, pl.ds(half * 16, 16)]

    def hops(half, way):
        return 4 if half == way else 3

    def send(o, hop):
        for half, way in ((0, 0), (1, 1), (1, 0), (0, 1)):
            length, sign = hops(half, way), 1 - 2 * way
            if hop >= length:
                continue
            if hop == 0:
                source = own(o, half, sign * length)
            else:
                source = r1.at[o, half, way, hop - 1]
                rcopy(
                    source, source, s_1.at[o, half, way, hop - 1], r_1.at[o, half, way, hop - 1], sibling
                ).wait_recv()
                source[...] = source[...] + own(o, half, sign * (length - hop))[...]
            rcopy(
                source, r1.at[o, half, way, hop], s_1.at[o, half, way, hop], r_1.at[o, half, way, hop],
                along("yz"[o], sign),
            ).start()

    def arrived(o, half):
        acc = own(o, half, 0)[...]
        for way in range(2):
            hop = hops(half, way) - 1
            ref = r1.at[o, half, way, hop]
            rcopy(ref, ref, s_1.at[o, half, way, hop], r_1.at[o, half, way, hop], sibling).wait_recv()
            acc = acc + ref[...]
        return acc

    def tile_sums(o):
        weights = jnp.concatenate([wk[i] for i in range(8)], axis=1)
        if o:
            weights = mm(swap, weights).astype(BF16)
        for n in range(2):
            part = mm(weights, qall[:, o * 512 + n * 256:o * 512 + (n + 1) * 256])
            acc2[o, :, :, n * 256:(n + 1) * 256] = part.reshape(8, 32, 256)

    def queries_half(half_at):
        cols = slice(half_at * 512, (half_at + 1) * 512)

        def passages(t, acc):
            at = pl.multiple_of(t * 256, 256)
            w = jnp.transpose(st[pl.ds(at, 256), :]).astype(BF16)
            return acc + mm(w, pall[pl.ds(at, 256), cols])

        def negatives(t, acc):
            at = pl.multiple_of(t * 256, 256)
            w = jnp.transpose(jnp.exp(hs[pl.ds(at, 256), :] - lse)).astype(BF16)
            return acc + mm(w, fn[pl.ds(at, 256), cols])

        acc = lax.fori_loop(0, NP // 256, passages, jnp.zeros((Q, 512), F32))
        acc = lax.fori_loop(0, SLOTS // 256, negatives, acc)
        gq_ref[:, cols] = acc

    queries_half(0)
    rcopy(side_rows, side_rows, s_q.at[1], r_q.at[1], sibling).wait_recv()
    rcopy(wk.at[pl.ds(0, 7)], wk.at[pl.ds(0, 7)], s_w, r_w, sibling).wait_recv()
    tile_sums(0)
    send(0, 0)
    tile_sums(1)
    send(1, 0)
    queries_half(1)
    for hop in range(1, 4):
        send(0, hop)
        send(1, hop)

    for o in range(2):
        b = "zy"[o]
        for half in range(2):
            acc = arrived(o, half)
            for i in range(4):
                a3[o, half * 4 + i] = acc[i * 4:(i + 1) * 4, :]
        for i in range(1, 8):
            rcopy(
                a3.at[o, (where[b] + i) % 8], r3.at[o, i - 1], s_3.at[o], r_3.at[o], along(b, i)
            ).start()

    for o in range(2):
        b = "zy"[o]
        rcopy(r3.at[o], r3.at[o], s_3.at[o], r_3.at[o], sibling).wait_recv()
        acc = a3[o, where[b]]
        for i in range(7):
            acc = acc + r3[o, i]
        gp_ref[:, o * 512:(o + 1) * 512] = acc

    def left(ref, sem):
        rcopy(ref, ref, sem, sem, sibling).wait_send()

    left(asked.at[pl.ds(0, NZ - 1)], s_req)
    left(reqin.at[pl.ds(0, 15)], s_pass)
    gone(CHUNKS - 2)
    gone(CHUNKS - 1)
    left(zbuf.at[pl.ds(0, NZ - 1)], s_ag.at[0])
    for n in range(2):
        for hop in range(4):
            left(pall.at[pl.ds(0, 16 if hop == 3 else 32)], s_y.at[n, hop])
    for n in range(2):
        left(pall.at[pl.ds(0, 256)], s_ag.at[2 + n])
        left(pall.at[pl.ds(0, 128)], s_ag.at[4 + n])
    left(pall.at[pl.ds(0, 1024)], s_ag.at[6])
    left(qall.at[pl.ds(0, (NX - 1) * Q)], s_q.at[0])
    left(side_rows, s_q.at[1])
    left(wk.at[pl.ds(0, 7)], s_w)
    for o in range(2):
        for half in range(2):
            for way in range(2):
                for hop in range(hops(half, way)):
                    left(r1.at[o, half, way, hop], s_1.at[o, half, way, hop])
        left(r3.at[o], s_3.at[o])


def shards(queries, passages, negatives, neg_ids, positives):
    vmem = pl.BlockSpec(memory_space=pltpu.VMEM)
    dma = pltpu.SemaphoreType.DMA
    req, slots = pl.pallas_call(
        requests,
        out_shape=(
            jax.ShapeDtypeStruct((NZ, 16, 1, 128), I32),
            jax.ShapeDtypeStruct((8, Q), I32),
        ),
        in_specs=[vmem],
        out_specs=(vmem, vmem),
    )(neg_ids.T)
    sums = pl.pallas_call(
        kernel,
        out_shape=(
            jax.ShapeDtypeStruct((Q, D), F32),
            jax.ShapeDtypeStruct((4, D), F32),
        ),
        in_specs=[vmem] * 6,
        out_specs=(vmem, vmem),
        scratch_shapes=[
            pltpu.VMEM((NZ, 16, 1, 128), I32),
            pltpu.VMEM((16, 1, 128), I32),
            pltpu.VMEM((16, 1, 128), I32),
            pltpu.SMEM((16, 1, 128), I32),
            pltpu.VMEM((ROWS, C8, 128), F32),
            pltpu.VMEM((NB * SLAB, 128), BF16),
            pltpu.VMEM((NB * SLAB, 128), BF16),
            pltpu.VMEM((PER * SLAB, 128), F32),
            pltpu.VMEM((SLOTS, D), BF16),
            pltpu.VMEM((NP, Q), F32),
            pltpu.VMEM((SLOTS, Q), F32),
            pltpu.VMEM((32, 128), F32),
            pltpu.VMEM((32, 128), BF16),
            pltpu.VMEM((NZ, 32, 128), BF16),
            pltpu.VMEM((NZ * 32, 128), F32),
            pltpu.VMEM((NP, D), BF16),
            pltpu.VMEM((8 * Q, D), BF16),
            pltpu.VMEM((8, 256, Q), BF16),
            pltpu.VMEM((8, 256, Q), BF16),
            pltpu.VMEM((2, 8, 32, 512), F32),
            pltpu.VMEM((2, 2, 2, 4, 16, 512), F32),
            pltpu.VMEM((2, 8, 4, 512), F32),
            pltpu.VMEM((2, 7, 4, 512), F32),
            dma, dma, dma((2, 4)), dma((CHUNKS,)), dma((7,)), dma, dma, dma((2, 4)), dma((GROUPS,)), dma((7,)),
            dma((2,)), dma((2,)), dma, dma,
            dma((2, 2, 2, 4)), dma((2, 2, 2, 4)), dma((2,)), dma((2,)), dma,
        ],
        compiler_params=pltpu.CompilerParams(
            collective_id=0, has_side_effects=True, vmem_limit_bytes=58 * 1024 * 1024
        ),
        cost_estimate=pl.CostEstimate(flops=4 * Q * NP * D * 2, bytes_accessed=1 << 24, transcendentals=0),
    )(req, slots, positives.reshape(1, Q), passages, queries, negatives)
    return pl.pallas_call(
        scaled,
        out_shape=(
            jax.ShapeDtypeStruct((Q, D), F32),
            jax.ShapeDtypeStruct((4, D), F32),
        ),
        in_specs=[vmem] * 2,
        out_specs=(vmem, vmem),
    )(*sums)


def solution(mesh):
    rows = P(("blk", "grp"), None)
    return jax.shard_map(
        shards,
        mesh=mesh,
        in_specs=(rows, rows, rows, rows, P(("blk", "grp"))),
        out_specs=(rows, rows),
        check_vma=False,
    )
```

```python
import functools
import math

import jax
import jax.numpy as jnp
from jax import lax
from jax.experimental import pallas as pl
from jax.experimental.pallas import tpu as pltpu
from jax.sharding import PartitionSpec as P

MESH = pl.DeviceIdType.MESH
F32, BF16, I32 = jnp.float32, jnp.bfloat16, jnp.int32

NX, NY, NZ, NYL = 4, 8, 8, 4
NB = 128
MUL, INV = 37, 45
CAP = 10
Q, D, HARD, ROWS = 128, 1024, 7, 896
C8 = D // 128
SLAB = CAP * C8
GROUPS = 8
PER = NB // GROUPS
CHUNKS = 16
STEPS = NB // CHUNKS
SLOTS = NB * CAP
NP = 2048
SCALE = 3.0 / math.sqrt(D)
NEG = -1e30


def device(x, y, z, core):
    return (((y % NYL) * NX + x) * NZ + z, (y // NYL) * 2 + core)


def rcopy(src, dst, send, recv, dev):
    return pltpu.make_async_remote_copy(
        src_ref=src, dst_ref=dst, send_sem=send, recv_sem=recv, device_id=dev, device_id_type=MESH
    )


def nt(left, right):
    return lax.dot_general(left, right, (((1,), (1,)), ((), ())), preferred_element_type=F32)


def mm(left, right):
    return lax.dot_general(left, right, (((1,), (0,)), ((), ())), preferred_element_type=F32)


def iota(shape, dim):
    return lax.broadcasted_iota(I32, shape, dim)


def requests(ids_ref, req, slots):
    mb = lax.axis_index("blk")
    sub = iota((128, Q), 0)
    before = (iota((Q, Q), 0) < iota((Q, Q), 1)).astype(F32).astype(BF16)
    base = jnp.zeros((NB, 1), F32)
    want_hi = jnp.zeros((NB, 128), F32)
    want_lo = jnp.zeros((NB, 128), F32)
    slots[...] = jnp.full((8, Q), -1, I32)
    for k in range(HARD):
        ids = ids_ref[k:k + 1, :]
        dev = jnp.floor((ids.astype(F32) + 0.5) * (1.0 / ROWS)).astype(I32)
        row = ids - dev * ROWS
        off = (dev >> 2) ^ mb
        kz, kxy = off & (NZ - 1), off >> 3
        step = (off * INV) & (NB - 1)
        hot = (sub == kz * 16 + kxy).astype(F32)
        hot16 = hot.astype(BF16)
        rank = jnp.sum(hot * (mm(hot16, before) + base), axis=0, keepdims=True).astype(I32)
        base = base + jnp.sum(hot, axis=1, keepdims=True)
        slots[k:k + 1, :] = step * CAP + rank
        at_lane = (sub == kz * 16 + rank).astype(F32)
        want_hi = want_hi + nt(hot16, (at_lane * (row >> 3).astype(F32)).astype(BF16))
        want_lo = want_lo + nt(hot16, (at_lane * (row & 7).astype(F32)).astype(BF16))
    req[...] = (want_hi * 8.0 + want_lo).astype(I32).reshape(NZ, 16, 1, 128)


def scaled(gq_in, gp_in, gq_ref, gp_ref):
    gq_ref[...] = gq_in[...] * SCALE
    gp_ref[...] = gp_in[...] * SCALE


def kernel(
    req, slots, pos_ref, pas_ref, q_ref, neg_ref,
    gq_ref, gp_ref,
    asked, passed, reqin, idsm, tab, g, f, fs, fn, st, hs, pst, pmine, zbuf, zf, pall,
    qall, posall, lseall, ts, wn, wh, wk, acc2, r1, a3, r3,
    s_req, s_pass, s_y, s_row, s_ag, r_req, r_pass, r_y, r_row, r_ag, s_q, r_q, s_w, r_w, s_p, r_p, s_1, r_1, s_3, r_3, s_loc,
):
    mb = lax.axis_index("blk")
    mg = lax.axis_index("grp")
    yl, x, z = mb // (NX * NZ), (mb // NZ) % NX, mb % NZ
    yh, core = mg // 2, mg % 2
    y = yh * NYL + yl

    def partner(step):
        return (mb ^ ((step * MUL) & (NB - 1)), mg)

    sibling = device(x, y, z, 1 - core)

    barrier = pltpu.get_barrier_semaphore()

    def greet(dev):
        pl.semaphore_signal(barrier, inc=1, device_id=dev, device_id_type=MESH)

    for i in range(1, NZ):
        greet((mb ^ i, mg))
    for n in range(1, 16):
        greet((mb ^ (n * NZ), mg))
    for i in range(NYL):
        greet(device(x, (1 - yh) * NYL + i, z, core))
    greet(sibling)
    for i in range(1, NX):
        greet(device((x + i) % NX, y, z, 1 - core))

    for c in range(C8):
        pst[pl.ds(c, 4, stride=C8), :] = pas_ref[:, c * 128:(c + 1) * 128].astype(F32)
    own = pst[...].astype(BF16)
    pmine[...] = own
    zbuf[z] = own

    pl.semaphore_wait(barrier, NZ - 1 + 15 + NYL + 1 + NX - 1)

    for i in range(1, NZ):
        rcopy(req.at[i], asked.at[i], s_req, r_req, (mb ^ i, mg)).start()
    asked[0] = req[0]

    for i in range(1, NZ):
        to = device(x, y, (z + i) % NZ, core)
        rcopy(pmine, zbuf.at[z], s_ag.at[0], r_ag.at[0], to).start()

    rcopy(asked.at[pl.ds(0, NZ - 1)], asked.at[pl.ds(0, NZ - 1)], s_req, r_req, sibling).wait_recv()
    total = asked[0]
    for i in range(1, NZ):
        total = total + asked[i]
    passed[...] = total
    for n in range(1, 16):
        rcopy(passed.at[n], reqin.at[n], s_pass, r_pass, (mb ^ (n * NZ), mg)).start()
    reqin[0] = passed[0]

    flat = tab.reshape(ROWS * C8, 128)
    for t in range(ROWS // 128):
        for c in range(C8):
            part = neg_ref[t * 128:(t + 1) * 128, c * 128:(c + 1) * 128].astype(F32)
            flat[pl.ds(t * 1024 + c, 128, stride=C8), :] = part

    rcopy(zbuf.at[pl.ds(0, NZ - 1)], zbuf.at[pl.ds(0, NZ - 1)], s_ag.at[0], r_ag.at[0], sibling).wait_recv()
    zf[...] = zbuf[...].reshape(NZ * 32, 128).astype(F32)
    mine = pl.multiple_of(((core * NX + x) * NY + y) * 32, 32)
    for c in range(C8):
        pall[pl.ds(mine, 32), c * 128:(c + 1) * 128] = zf[pl.ds(c, 32, stride=C8), :].astype(BF16)

    def along_y(hop):
        for n in range(2):
            sign = 1 - 2 * n
            rows = 16 if hop == 3 else 32
            at = ((core * NX + x) * NY + (y + NY - sign * hop) % NY) * 32 + (16 * n if hop == 3 else 0)
            block = pall.at[pl.ds(pl.multiple_of(at, 16), rows)]
            if hop:
                came = pall.at[pl.ds(0, 32)]
                rcopy(came, came, s_y.at[n, hop - 1], r_y.at[n, hop - 1], sibling).wait_recv()
            to = device(x, (y + NY + sign) % NY, z, core)
            rcopy(block, block, s_y.at[n, hop], r_y.at[n, hop], to).start()

    along_y(0)

    rcopy(reqin.at[pl.ds(0, 15)], reqin.at[pl.ds(0, 15)], s_pass, r_pass, sibling).wait_recv()
    local = pltpu.make_async_copy(reqin, idsm, s_loc)
    local.start()
    local.wait()

    def pick(step, dst):
        at = pl.multiple_of(step * SLAB, 16)
        k = (step * MUL) % NB
        n, lane = k // NZ, (k % NZ) * 16
        for j in range(CAP // 2):
            pair = jnp.concatenate([tab[idsm[n, 0, lane + 2 * j]], tab[idsm[n, 0, lane + 2 * j + 1]]], axis=0)
            dst[pl.ds(at + 16 * j, 16), :] = pair.astype(BF16)

    def answer(step, _):
        pick(step, g)
        at = pl.multiple_of(step * SLAB, 16)
        rcopy(
            g.at[pl.ds(at, SLAB)], f.at[pl.ds(at, SLAB)], s_row.at[step // STEPS], r_row.at[step // PER], partner(step)
        ).start()
        return 0

    def gone(chunk):
        ref = f.at[pl.ds(0, (STEPS - (1 if chunk == 0 else 0)) * SLAB)]
        rcopy(ref, ref, s_row.at[chunk], s_row.at[chunk], sibling).wait_send()

    def answers(chunk):
        lax.fori_loop(max(1, chunk * STEPS), (chunk + 1) * STEPS, answer, 0)
        if chunk >= 2:
            gone(chunk - 2)

    right, left_x = device((x + 1) % NX, y, z, core), device((x + NX - 1) % NX, y, z, core)

    def slab(at, rows, extra=0):
        return pall.at[pl.ds(pl.multiple_of((core * NX + at) * 256 + extra, 128), rows)]

    def along_x(hop):
        for n, to in ((0, right), (1, left_x)):
            if hop == 0:
                came = pall.at[pl.ds(0, 16)]
                rcopy(came, came, s_y.at[n, 3], r_y.at[n, 3], sibling).wait_recv()
        for n, to in ((0, right), (1, left_x)):
            if hop == 0:
                rcopy(slab(x, 256), slab(x, 256), s_ag.at[2 + n], r_ag.at[2 + n], to).start()
            else:
                came = (x + NX - 1) % NX if n == 0 else (x + 1) % NX
                rcopy(slab(came, 256), slab(came, 256), s_ag.at[2 + n], r_ag.at[2 + n], to).wait_recv()
                part = slab(came, 128, 128 * n)
                rcopy(part, part, s_ag.at[4 + n], r_ag.at[4 + n], to).start()

    half = pall.at[pl.ds(pl.multiple_of(core * 1024, 1024), 1024)]

    def across():
        for n in range(2):
            part = slab((x + 2) % NX, 128, 128 * n)
            rcopy(part, part, s_ag.at[4 + n], r_ag.at[4 + n], sibling).wait_recv()
        rcopy(half, half, s_ag.at[6], r_ag.at[6], sibling).start()

    def score(t, top):
        at = pl.multiple_of(t * 256, 256)
        part = nt(pall[pl.ds(at, 256), :], q_ref[...]) * SCALE
        st[pl.ds(at, 256), :] = part
        return jnp.maximum(top, jnp.max(part, axis=0, keepdims=True))

    def raise_(t, carry):
        pool_top, total = carry
        at = pl.multiple_of(t * 256, 256)
        part = jnp.exp(st[pl.ds(at, 256), :] - pool_top)
        st[pl.ds(at, 256), :] = part
        return pool_top, total + jnp.sum(part, axis=0, keepdims=True)

    def pool():
        rcopy(half, half, s_ag.at[6], r_ag.at[6], sibling).wait_recv()
        pool_top = lax.fori_loop(0, NP // 256, score, jnp.full((1, Q), NEG, F32))
        return lax.fori_loop(0, NP // 256, raise_, (pool_top, jnp.zeros((1, Q), F32)))

    def hard(group, top):
        at = pl.multiple_of(group * PER * SLAB, PER * SLAB)
        row0 = pl.multiple_of(group * PER * CAP, PER * CAP)
        fs[...] = f[pl.ds(at, PER * SLAB), :].astype(F32)
        for c in range(C8):
            fn[pl.ds(row0, PER * CAP), c * 128:(c + 1) * 128] = fs[
                pl.ds(c, PER * CAP, stride=C8), :
            ].astype(BF16)
        part = nt(fn[pl.ds(row0, PER * CAP), :], q_ref[...]) * SCALE
        number = iota((PER * CAP, Q), 0) + row0
        taken = number == slots[0:1, :]
        for k in range(1, HARD):
            taken = taken | (number == slots[k:k + 1, :])
        part = jnp.where(taken, part, NEG)
        hs[pl.ds(row0, PER * CAP), :] = part
        return jnp.maximum(top, jnp.max(part, axis=0, keepdims=True))

    def group_in(group, top):
        n = PER - (1 if group == 0 else 0)
        ref = f.at[pl.ds(0, n * SLAB)]
        rcopy(ref, ref, s_pass, r_row.at[group], sibling).wait_recv()
        return hard(group, top)

    p = pos_ref[...]
    answer_slot = (
        (((p >> 2) & 1) << 10)
        | (((p >> 7) & 3) << 8)
        | (((p >> 3) & 1) << 7)
        | (((p >> 9) & 3) << 5)
        | (((p >> 4) & 7) << 2)
        | (p & 3)
    )
    own_slot = core * NX + x
    own_rows = qall.at[pl.ds(pl.multiple_of(own_slot * Q, Q), Q)]
    own_rows[...] = q_ref[...]
    posall[own_slot] = jnp.broadcast_to(answer_slot, (8, Q))

    def to_eight(ref, s_sem, r_sem):
        for dc, dx in ((1, 2), (0, 2), (1, 1), (1, 3), (0, 1), (0, 3), (1, 0)):
            to = device((x + dx) % NX, y, z, (core + dc) % 2)
            rcopy(ref.at[own_slot], ref.at[own_slot], s_sem, r_sem, to).start()

    def from_eight(ref, s_sem, r_sem):
        rcopy(ref.at[pl.ds(0, 7)], ref.at[pl.ds(0, 7)], s_sem, r_sem, sibling).wait_recv()

    def queries_x():
        for i in range(1, NX):
            to = device((x + i) % NX, y, z, core)
            rcopy(own_rows, own_rows, s_q.at[0], r_q.at[0], to).start()
        to_eight(posall, s_p, r_p)

    side_rows = qall.at[pl.ds(pl.multiple_of(core * NX * Q, NX * Q), NX * Q)]

    def queries_across():
        ref = qall.at[pl.ds(0, (NX - 1) * Q)]
        rcopy(ref, ref, s_q.at[0], r_q.at[0], sibling).wait_recv()
        rcopy(side_rows, side_rows, s_q.at[1], r_q.at[1], sibling).start()

    def tile_scores():
        rcopy(side_rows, side_rows, s_q.at[1], r_q.at[1], sibling).wait_recv()

        def one(i, _):
            tile = pall[pl.ds(pl.multiple_of(own_slot * 256, 256), 256), :]
            ts[i] = nt(tile, qall[pl.ds(pl.multiple_of(i * Q, Q), Q), :]) * SCALE
            return 0

        lax.fori_loop(0, 8, one, 0)

    hard_top = jnp.full((1, Q), NEG, F32)
    along_y(1)
    for chunk in range(CHUNKS):
        answers(chunk)
        if chunk == 0:
            pick(0, f)
            along_y(2)
        elif chunk == 1:
            along_y(3)
        elif chunk == 2:
            along_x(0)
        elif chunk == 5:
            along_x(1)
        elif chunk == 7:
            across()
        elif chunk == 10:
            pool_top, pool_total = pool()
        elif chunk == 6:
            queries_x()
        elif chunk == 12:
            queries_across()
        elif chunk == 15:
            tile_scores()
        if chunk >= 5 and chunk % 2 == 1:
            hard_top = group_in((chunk - 5) // 2, hard_top)
    for group in range((CHUNKS - 4) // 2, GROUPS):
        hard_top = group_in(group, hard_top)
    top = jnp.maximum(pool_top, hard_top)

    total = pool_total * jnp.exp(pool_top - top) + jnp.sum(jnp.exp(hs[...] - top), axis=0, keepdims=True)
    lse = top + jnp.log(total)
    factor = jnp.exp(pool_top - lse)

    there = iota((256, 256), 0)
    source = (((there >> 2) & 7) << 5) | ((there >> 5) << 2) | (there & 3)
    swap = (iota((256, 256), 1) == source).astype(F32).astype(BF16)

    lseall[own_slot] = jnp.broadcast_to(lse, (8, Q))
    to_eight(lseall, s_w, r_w)

    def turn(t, _):
        at = pl.multiple_of(t * 256, 256)
        hit = (iota((256, Q), 0) + at == answer_slot).astype(F32)
        w = st[pl.ds(at, 256), :] * factor - hit
        wn[:, pl.ds(at, 256)] = jnp.transpose(w).astype(BF16)
        return 0

    def turn_hard(t, _):
        at = pl.multiple_of(t * 256, 256)
        w = jnp.exp(hs[pl.ds(at, 256), :] - lse)
        wh[:, pl.ds(at, 256)] = jnp.transpose(w).astype(BF16)
        return 0

    lax.fori_loop(0, NP // 256, turn, 0)
    from_eight(posall, s_p, r_p)
    from_eight(lseall, s_w, r_w)

    def weigh(i, _):
        hit = (iota((256, Q), 0) + own_slot * 256 == posall[i, 0:1, :]).astype(F32)
        wk[i] = (jnp.exp(ts[i] - lseall[i, 0:1, :]) - hit).astype(BF16)
        return 0

    lax.fori_loop(0, 8, weigh, 0)

    def along(axis, i):
        return (
            device((x + i + NX) % NX, y, z, core) if axis == "x"
            else device(x, (y + i + NY) % NY, z, core) if axis == "y"
            else device(x, y, (z + i + NZ) % NZ, core)
        )

    where = {"y": y, "z": z}

    def own(o, half, target):
        return acc2.at[o, (where["yz"[o]] + target + 8) % 8, pl.ds(half * 16, 16)]

    def hops(half, way):
        return 4 if half == way else 3

    def send(o, hop):
        for half, way in ((0, 0), (1, 1), (1, 0), (0, 1)):
            length, sign = hops(half, way), 1 - 2 * way
            if hop >= length:
                continue
            if hop == 0:
                source = own(o, half, sign * length)
            else:
                source = r1.at[o, half, way, hop - 1]
                rcopy(
                    source, source, s_1.at[o, half, way, hop - 1], r_1.at[o, half, way, hop - 1], sibling
                ).wait_recv()
                source[...] = source[...] + own(o, half, sign * (length - hop))[...]
            rcopy(
                source, r1.at[o, half, way, hop], s_1.at[o, half, way, hop], r_1.at[o, half, way, hop],
                along("yz"[o], sign),
            ).start()

    def arrived(o, half):
        acc = own(o, half, 0)[...]
        for way in range(2):
            hop = hops(half, way) - 1
            ref = r1.at[o, half, way, hop]
            rcopy(ref, ref, s_1.at[o, half, way, hop], r_1.at[o, half, way, hop], sibling).wait_recv()
            acc = acc + ref[...]
        return acc

    def tile_sums(o):
        weights = jnp.concatenate([wk[i] for i in range(8)], axis=1)
        if o:
            weights = mm(swap, weights).astype(BF16)
        for n in range(2):
            part = mm(weights, qall[:, o * 512 + n * 256:o * 512 + (n + 1) * 256])
            acc2[o, :, :, n * 256:(n + 1) * 256] = part.reshape(8, 32, 256)

    def queries_half(half_at):
        cols = slice(half_at * 512, (half_at + 1) * 512)

        def passages(t, acc):
            at = pl.multiple_of(t * 256, 256)
            return acc + mm(wn[:, pl.ds(at, 256)], pall[pl.ds(at, 256), cols])

        def negatives(t, acc):
            at = pl.multiple_of(t * 256, 256)
            return acc + mm(wh[:, pl.ds(at, 256)], fn[pl.ds(at, 256), cols])

        acc = lax.fori_loop(0, NP // 256, passages, jnp.zeros((Q, 512), F32))
        acc = lax.fori_loop(0, SLOTS // 256, negatives, acc)
        gq_ref[:, cols] = acc

    tile_sums(0)
    send(0, 0)
    tile_sums(1)
    send(1, 0)
    lax.fori_loop(0, SLOTS // 256, turn_hard, 0)
    queries_half(0)
    send(0, 1)
    send(1, 1)
    queries_half(1)
    for hop in range(2, 4):
        send(0, hop)
        send(1, hop)

    for o in range(2):
        b = "zy"[o]
        for half in range(2):
            acc = arrived(o, half)
            for i in range(4):
                a3[o, half * 4 + i] = acc[i * 4:(i + 1) * 4, :]
        for i in range(1, 8):
            rcopy(
                a3.at[o, (where[b] + i) % 8], r3.at[o, i - 1], s_3.at[o], r_3.at[o], along(b, i)
            ).start()

    for o in range(2):
        b = "zy"[o]
        rcopy(r3.at[o], r3.at[o], s_3.at[o], r_3.at[o], sibling).wait_recv()
        acc = a3[o, where[b]]
        for i in range(7):
            acc = acc + r3[o, i]
        gp_ref[:, o * 512:(o + 1) * 512] = acc

    def left(ref, sem):
        rcopy(ref, ref, sem, sem, sibling).wait_send()

    left(asked.at[pl.ds(0, NZ - 1)], s_req)
    left(reqin.at[pl.ds(0, 15)], s_pass)
    gone(CHUNKS - 2)
    gone(CHUNKS - 1)
    left(zbuf.at[pl.ds(0, NZ - 1)], s_ag.at[0])
    for n in range(2):
        for hop in range(4):
            left(pall.at[pl.ds(0, 16 if hop == 3 else 32)], s_y.at[n, hop])
    for n in range(2):
        left(pall.at[pl.ds(0, 256)], s_ag.at[2 + n])
        left(pall.at[pl.ds(0, 128)], s_ag.at[4 + n])
    left(pall.at[pl.ds(0, 1024)], s_ag.at[6])
    left(qall.at[pl.ds(0, (NX - 1) * Q)], s_q.at[0])
    left(side_rows, s_q.at[1])
    left(lseall.at[pl.ds(0, 7)], s_w)
    left(posall.at[pl.ds(0, 7)], s_p)
    for o in range(2):
        for half in range(2):
            for way in range(2):
                for hop in range(hops(half, way)):
                    left(r1.at[o, half, way, hop], s_1.at[o, half, way, hop])
        left(r3.at[o], s_3.at[o])


def shards(queries, passages, negatives, neg_ids, positives):
    vmem = pl.BlockSpec(memory_space=pltpu.VMEM)
    dma = pltpu.SemaphoreType.DMA
    req, slots = pl.pallas_call(
        requests,
        out_shape=(
            jax.ShapeDtypeStruct((NZ, 16, 1, 128), I32),
            jax.ShapeDtypeStruct((8, Q), I32),
        ),
        in_specs=[vmem],
        out_specs=(vmem, vmem),
    )(neg_ids.T)
    sums = pl.pallas_call(
        kernel,
        out_shape=(
            jax.ShapeDtypeStruct((Q, D), F32),
            jax.ShapeDtypeStruct((4, D), F32),
        ),
        in_specs=[vmem] * 6,
        out_specs=(vmem, vmem),
        scratch_shapes=[
            pltpu.VMEM((NZ, 16, 1, 128), I32),
            pltpu.VMEM((16, 1, 128), I32),
            pltpu.VMEM((16, 1, 128), I32),
            pltpu.SMEM((16, 1, 128), I32),
            pltpu.VMEM((ROWS, C8, 128), F32),
            pltpu.VMEM((NB * SLAB, 128), BF16),
            pltpu.VMEM((NB * SLAB, 128), BF16),
            pltpu.VMEM((PER * SLAB, 128), F32),
            pltpu.VMEM((SLOTS, D), BF16),
            pltpu.VMEM((NP, Q), F32),
            pltpu.VMEM((SLOTS, Q), F32),
            pltpu.VMEM((32, 128), F32),
            pltpu.VMEM((32, 128), BF16),
            pltpu.VMEM((NZ, 32, 128), BF16),
            pltpu.VMEM((NZ * 32, 128), F32),
            pltpu.VMEM((NP, D), BF16),
            pltpu.VMEM((8 * Q, D), BF16),
            pltpu.VMEM((8, 8, Q), I32),
            pltpu.VMEM((8, 8, Q), F32),
            pltpu.VMEM((8, 256, Q), F32),
            pltpu.VMEM((Q, NP), BF16),
            pltpu.VMEM((Q, SLOTS), BF16),
            pltpu.VMEM((8, 256, Q), BF16),
            pltpu.VMEM((2, 8, 32, 512), F32),
            pltpu.VMEM((2, 2, 2, 4, 16, 512), F32),
            pltpu.VMEM((2, 8, 4, 512), F32),
            pltpu.VMEM((2, 7, 4, 512), F32),
            dma, dma, dma((2, 4)), dma((CHUNKS,)), dma((7,)), dma, dma, dma((2, 4)), dma((GROUPS,)), dma((7,)),
            dma((2,)), dma((2,)), dma, dma, dma, dma,
            dma((2, 2, 2, 4)), dma((2, 2, 2, 4)), dma((2,)), dma((2,)), dma,
        ],
        compiler_params=pltpu.CompilerParams(
            collective_id=0, has_side_effects=True, vmem_limit_bytes=58 * 1024 * 1024
        ),
        cost_estimate=pl.CostEstimate(flops=4 * Q * NP * D * 2, bytes_accessed=1 << 24, transcendentals=0),
    )(req, slots, positives.reshape(1, Q), passages, queries, negatives)
    return pl.pallas_call(
        scaled,
        out_shape=(
            jax.ShapeDtypeStruct((Q, D), F32),
            jax.ShapeDtypeStruct((4, D), F32),
        ),
        in_specs=[vmem] * 2,
        out_specs=(vmem, vmem),
    )(*sums)


def solution(mesh):
    rows = P(("blk", "grp"), None)
    return jax.shard_map(
        shards,
        mesh=mesh,
        in_specs=(rows, rows, rows, rows, P(("blk", "grp"))),
        out_specs=(rows, rows),
        check_vma=False,
    )
```
